512 devices in a mesh: seq: 32 (over y, z_hi, core), chan: 16 (over x, z_lo).
Axes of the slice: x: 4, y: 4, z: 16 (z_hi: 4, z_lo: 4; z = z_hi * 4 + z_lo), core: 2. Of those that a mesh axis runs over, the one named last changes fastest.
Arguments:
- outer_gate: bfloat16 [16384, 2048], P('seq', 'chan'), may hold values from -6 to 6
- inner_gate: bfloat16 [16384, 2048], P('seq', 'chan'), may hold values from -6 to 6
- values: bfloat16 [16384, 2048], P('seq', 'chan'), may hold values from -6 to 6
- filters: bfloat16 [16384, 16], P('seq'), may hold values from -0.046875 to 0.046875
- cotangent: bfloat16 [16384, 2048], P('seq', 'chan'), may hold values from -6 to 6
Outputs:
- layer_out: bfloat16 [16384, 2048], P('seq', 'chan')
- outer_grad: bfloat16 [16384, 2048], P('seq', 'chan')
- inner_grad: bfloat16 [16384, 2048], P('seq', 'chan')
- value_grad: bfloat16 [16384, 2048], P('seq', 'chan')
- filter_grad: float32 [16384, 16], P('seq')
The draws below stay inside these ranges and needn't reach their ends.
All inputs are finite; a program needn't handle non-finite values.
Results may differ from the reference program's by a relative error of at most 0.0051.
Values may be sent and summed in bfloat16 or wider, within the bound.
A program may use at most 128 MiB of HBM per device.

```python
import jax
import jax.numpy as jnp
from jax import lax

CH_DEV = 128
FILTERS = 16
TOKENS = 16384
CHANNELS = 2048
N_CHAN = 16


def levels(rng, dims, cuts, low, largest):
    level, own = 1.0, jax.random.fold_in(rng, 6)
    for axis_at, shards_of in cuts:
        heights = jnp.exp(jax.random.uniform(jax.random.fold_in(own, axis_at), (shards_of,), jnp.float32, low / len(cuts), largest / len(cuts)))
        level = level * jnp.repeat(heights, dims[axis_at] // shards_of).reshape([-1 if axis == axis_at else 1 for axis in range(len(dims))])
    return level


def normal_values(key, extent, scale, limit, pieces=(), kind=jnp.bfloat16):
    loudness = levels(key, extent, pieces, -0.22, 0.18) if pieces else 1.0
    values = jax.random.normal(key, extent, jnp.float32) * scale * loudness
    return jnp.minimum(jnp.maximum(values, -limit), limit).astype(kind)


def setup_inputs(seed: int = 0) -> dict:
    key_list = jax.random.split(jax.random.key(seed), 6)
    return {
        "outer_gate": normal_values(key_list[0], (TOKENS, CHANNELS), 1.0, 6.0, ((0, 32), (1, 16))),
        "inner_gate": normal_values(key_list[1], (TOKENS, CHANNELS), 1.0, 6.0, ((0, 32), (1, 16))),
        "values": normal_values(key_list[2], (TOKENS, CHANNELS), 1.0, 6.0, ((0, 32), (1, 16))),
        "filters": normal_values(key_list[3], (TOKENS, FILTERS), TOKENS ** -0.5, 0.046875, ((0, 32),)),
        "cotangent": normal_values(key_list[4], (TOKENS, CHANNELS), 1.0, 6.0, ((0, 32), (1, 16))),
    }


def reference(outer_gate, inner_gate, values, filters, cotangent):
    tokens = outer_gate.shape[0]
    length = 2 * tokens
    inner = (inner_gate.astype(jnp.float32) * values.astype(jnp.float32)).astype(jnp.bfloat16)
    upstream = (cotangent.astype(jnp.float32) * outer_gate.astype(jnp.float32)).astype(jnp.bfloat16)
    filter_spec = jnp.fft.rfft(filters.astype(jnp.float32), n=length, axis=0)
    copies = CH_DEV // FILTERS
    tiled_spec = jnp.tile(filter_spec, (1, copies))

    def one_group(total, group):
        start = (group * CH_DEV).astype(jnp.int32)
        inner_block = lax.dynamic_slice_in_dim(inner, start, CH_DEV, 1).astype(jnp.float32)
        upper_block = lax.dynamic_slice_in_dim(upstream, start, CH_DEV, 1).astype(jnp.float32)
        inner_spec = jnp.fft.rfft(inner_block, n=length, axis=0)
        upper_spec = jnp.fft.rfft(upper_block, n=length, axis=0)
        convolved = jnp.fft.irfft(tiled_spec * inner_spec, n=length, axis=0)[:tokens]
        backward = jnp.fft.irfft(jnp.conj(tiled_spec) * upper_spec, n=length, axis=0)[:tokens]
        correlated = jnp.fft.irfft(jnp.conj(inner_spec) * upper_spec, n=length, axis=0)[:tokens]
        total = total + correlated.reshape(tokens, copies, FILTERS).sum(axis=1)
        return total, (convolved, backward)

    start_total = jnp.zeros((tokens, FILTERS), jnp.float32)
    total, (conv_blocks, back_blocks) = lax.scan(one_group, start_total, jnp.arange(N_CHAN, dtype=jnp.int32))
    channels = outer_gate.shape[1]
    convolved = jnp.transpose(conv_blocks, (1, 0, 2)).reshape(tokens, channels)
    backward = jnp.transpose(back_blocks, (1, 0, 2)).reshape(tokens, channels)
    layer_out = (outer_gate.astype(jnp.float32) * convolved).astype(jnp.bfloat16)
    outer_grad = (cotangent.astype(jnp.float32) * convolved).astype(jnp.bfloat16)
    inner_grad = (backward * values.astype(jnp.float32)).astype(jnp.bfloat16)
    value_grad = (backward * inner_gate.astype(jnp.float32)).astype(jnp.bfloat16)
    grad_scale = float(tokens * channels // FILTERS) ** -0.5
    filter_grad = total * grad_scale
    return layer_out, outer_grad, inner_grad, value_grad, filter_grad
```

```python
import jax
import jax.numpy as jnp
from jax import lax
from jax.experimental import pallas as pl
from jax.experimental.pallas import tpu as pltpu
from jax.sharding import PartitionSpec as P

BF16 = jnp.bfloat16
F32 = jnp.float32
MESH = pl.DeviceIdType.MESH
SEQ = 32
CHAN = 16
TAPS = 16
LANES = 128
ROWS = 256


def nn(a, b):
    return lax.dot_general(a, b, (((1,), (0,)), ((), ())), preferred_element_type=F32)


def nt(a, b):
    return lax.dot_general(a, b, (((1,), (1,)), ((), ())), preferred_element_type=F32)


def iota(shape, axis):
    return lax.broadcasted_iota(jnp.int32, shape, axis)


def one_hot(hit):
    return jnp.where(hit, 1.0, 0.0).astype(BF16)


def eye(n):
    return one_hot(iota((n, n), 0) == iota((n, n), 1))


def flip(n):
    return one_hot(iota((n, n), 0) + iota((n, n), 1) == n - 1)


def routing():
    row, col = iota((512, 512), 0), iota((512, 512), 1)
    s, p, b, k = row >> 4, (row >> 3) & 1, (row >> 2) & 1, row & 3
    wanted = (2 * b + 1 - p) * LANES + (s >> 1) + TAPS * (4 * (s & 1) + k)
    return one_hot(col == wanted)


def stack_tokens(x, order):
    return jnp.concatenate([x[LANES * n : LANES * (n + 1)] for n in order], axis=1)


def shear(x):
    return pltpu.roll(x, 0, 1, stride=1, stride_axis=0)


def upper():
    return iota((LANES, LANES), 1) >= iota((LANES, LANES), 0)


def toeplitz(taps, w):
    w[0:LANES, :] = jnp.zeros((LANES, LANES), BF16)
    keep = upper()

    def body(s, before):
        for n in range(4):
            h = taps[s, n : n + 1, :].astype(F32)
            now = shear(jnp.broadcast_to(h, (LANES, LANES)))
            at = pl.multiple_of((4 * s + n + 1) * LANES, LANES)
            w[pl.ds(at, LANES), :] = jnp.where(keep, now, before).astype(BF16)
            before = now
        return before

    lax.fori_loop(0, SEQ, body, jnp.zeros((LANES, LANES), F32))


def unpack(slots):
    wide = slots[...].astype(F32)
    return jnp.concatenate(
        [wide[:, 0:8].reshape(ROWS, LANES), wide[:, 8:16].reshape(ROWS, LANES)], axis=1
    )


def pack(y):
    return jnp.concatenate(
        [y[:, :LANES].reshape(SEQ, 8, LANES), y[:, LANES:].reshape(SEQ, 8, LANES)], axis=1
    ).astype(BF16)


def spread_x(x, xs):
    xs[0:ROWS, :] = jnp.zeros((ROWS, 1024), BF16)
    row = iota((ROWS, ROWS), 0)
    for d in range(4):
        moved = x if d == 0 else jnp.where(row >= 4 * d, pltpu.roll(x, 4 * d, 0), 0.0)
        xs[ROWS:, ROWS * d : ROWS * (d + 1)] = moved.astype(BF16)


def spread_u(u, us):
    us[ROWS:, :] = jnp.zeros((us.shape[0] - ROWS, 1024), BF16)
    row = iota((ROWS, ROWS), 0)
    for d in range(4):
        moved = u if d == 0 else jnp.where(row < ROWS - 4 * d, pltpu.roll(u, ROWS - 4 * d, 0), 0.0)
        us[0:ROWS, ROWS * d : ROWS * (d + 1)] = moved.astype(BF16)


def lag_weights(w, group):
    at = pl.multiple_of(group * 1024, 1024)
    return jnp.concatenate(
        [w[pl.ds(at, 1024), :], w[pl.ds(pl.multiple_of(at + LANES, LANES), 1024), :]], axis=1
    )


def convolve(xs, w, y):
    y[...] = jnp.zeros((ROWS, ROWS), F32)
    for quarter in range(4):
        size = ROWS - 64 * quarter

        def body(g, _):
            at = pl.multiple_of(ROWS - 16 * g, 16)
            y[64 * quarter :, :] += nn(xs[pl.ds(at, size), :], lag_weights(w, 4 * quarter + g))
            return 0

        lax.fori_loop(0, 4, body, 0)


def convolve_back(us, w, y):
    y[...] = jnp.zeros((ROWS, ROWS), F32)
    for quarter in range(4):
        size = ROWS - 64 * quarter

        def body(g, _):
            group = 4 * quarter + g
            at = pl.multiple_of(16 * group, 16)
            y[0:size, :] += nn(us[pl.ds(at, size), :], lag_weights(w, group))
            return 0

        lax.fori_loop(0, 4, body, 0)


def correlate(ut, xs, out):
    keep = upper()

    def emit(before, now, group, e):
        line = jnp.sum(jnp.where(keep, before, now), axis=0, keepdims=True)
        out[2 * group + (e + 6) // 4, (e + 6) % 4, :] = line[0]

    def body(group, carry):
        before, edge = carry
        at = pl.multiple_of(ROWS - 16 * group, 16)
        pairs = nn(ut[...], xs[pl.ds(at, ROWS), :])
        for e in range(8):
            low = pairs[0:LANES, LANES * e : LANES * (e + 1)]
            high = edge if e == 0 else pairs[LANES:, LANES * (e - 1) : LANES * e]
            now = shear(low + high)
            emit(before, now, group, e)
            before = now
        return before, pairs[LANES:, LANES * 7 :]

    zero = jnp.zeros((LANES, LANES), F32)
    before, edge = lax.fori_loop(0, 16, body, (zero, zero))
    now = shear(edge)
    emit(before, now, 16, 0)
    emit(now, zero, 16, 1)


def product(a, b):
    return a[...].astype(F32) * b[...].astype(F32)


def kernel(
    og, ig, va, taps, ct,
    layer_out, outer_grad, inner_grad, value_grad, filter_grad,
    send_h, send_x, send_u, send_c, send_b, send_g, send_t,
    recv_h, recv_x, recv_u, recv_c, recv_b, recv_g, recv_t,
    w, xs, us, ut, y, route, sems_out, sems_in,
):
    s, c = lax.axis_index("seq"), lax.axis_index("chan")
    f, half = s // 2, s % 2
    own_part = 16 * half + c
    is_self = s == own_part

    def device(seq, chan):
        return {"seq": seq, "chan": chan}

    barrier = pltpu.get_barrier_semaphore()

    def greet(seq, chan):
        pl.semaphore_signal(barrier, inc=1, device_id=device(seq, chan), device_id_type=MESH)

    def greet_seq(i, _):
        greet(lax.rem(s + i, SEQ), c)
        return 0

    def greet_chan(i, _):
        greet(s, lax.rem(c + i, CHAN))
        greet(2 * f + 1 - half, lax.rem(c + i, CHAN))
        return 0

    def greet_source(i, _):
        @pl.when(jnp.logical_not(jnp.logical_and(is_self, i == f)))
        def _():
            greet(2 * i + s // 16, lax.rem(s, 16))

        return 0

    lax.fori_loop(1, SEQ, greet_seq, 0)
    lax.fori_loop(1, CHAN, greet_chan, 0)
    greet(2 * f + 1 - half, c)
    lax.fori_loop(0, TAPS, greet_source, 0)

    taps_flat = stack_tokens(taps[...], range(4))
    row, col = iota((64, 64), 0), iota((64, 64), 1)
    taps_rows = nt(one_hot(col == (row & 3) * TAPS + (row >> 2)), taps_flat).astype(BF16)
    for i in range(TAPS):
        send_h[i] = taps_rows[4 * i : 4 * (i + 1)]
    route[...] = routing()
    inner = stack_tokens(product(ig, va).astype(BF16), range(4))
    send_x[...] = nt(route[...], inner).astype(BF16).reshape(SEQ, 16, LANES)
    upstream = stack_tokens(product(ct, og).astype(BF16), (1, 0, 3, 2))
    upstream = nn(flip(LANES), upstream).astype(BF16)
    send_u[...] = nt(route[...], upstream).astype(BF16).reshape(SEQ, 16, LANES)

    @pl.when(is_self)
    def _():
        pl.semaphore_wait(barrier, 2 * (SEQ - 1) + TAPS - 1)

    @pl.when(jnp.logical_not(is_self))
    def _():
        pl.semaphore_wait(barrier, 2 * (SEQ - 1) + TAPS)

    def copy(src, dst, n, seq, chan):
        return pltpu.make_async_remote_copy(
            src_ref=src, dst_ref=dst, send_sem=sems_out.at[n], recv_sem=sems_in.at[n],
            device_id=device(seq, chan), device_id_type=MESH,
        )

    def exchange(src, dst, n, slot):
        def body(i, _):
            to = lax.rem(s + i, SEQ)
            copy(src.at[slot(to)], dst.at[s], n, to, c).start()
            return 0

        lax.fori_loop(1, SEQ, body, 0)
        dst[s] = src[slot(s)]

    def whole(ref, count, n):
        part = ref.at[pl.ds(0, count)]
        return copy(part, part, n, s, c)

    exchange(send_h, recv_h, 0, lambda to: to // 2)
    exchange(send_x, recv_x, 1, lambda to: to)
    exchange(send_u, recv_u, 2, lambda to: to)

    whole(recv_h, SEQ - 1, 0).wait_recv()
    toeplitz(recv_h, w)
    whole(recv_x, SEQ - 1, 1).wait_recv()
    spread_x(unpack(recv_x), xs)
    convolve(xs, w, y)
    send_c[...] = pack(y[...])
    exchange(send_c, recv_c, 3, lambda to: to)

    whole(recv_u, SEQ - 1, 2).wait_recv()
    u = unpack(recv_u)
    spread_u(u, us)
    ut[...] = nt(eye(ROWS), u.astype(BF16)).astype(BF16)
    convolve_back(us, w, y)
    send_b[...] = pack(y[...])
    exchange(send_b, recv_b, 4, lambda to: to)

    correlate(ut, xs, send_g)

    def parts_out(i, _):
        to = lax.rem(c + i, CHAN)
        here = c * 2 + half

        @pl.when(i > 0)
        def _():
            copy(send_g.at[2 + 16 * half + to], recv_g.at[here], 5, s, to).start()

        other = 1 - half
        copy(send_g.at[2 + 16 * other + to], recv_g.at[here], 5, 2 * f + other, to).start()
        return 0

    lax.fori_loop(0, CHAN, parts_out, 0)
    recv_g[c * 2 + half] = send_g[2 + own_part]

    whole(recv_c, SEQ - 1, 3).wait_recv()
    tokens = nt(eye(LANES), recv_c[...].reshape(512, LANES)).astype(BF16)
    result = nn(tokens, route[...])
    for n in range(4):
        here = pl.ds(LANES * (n ^ 1), LANES)
        part = result[:, LANES * n : LANES * (n + 1)]
        layer_out[here, :] = (og[here, :].astype(F32) * part).astype(BF16)
        outer_grad[here, :] = (ct[here, :].astype(F32) * part).astype(BF16)

    whole(recv_g, SEQ - 1, 5).wait_recv()
    send_t[0] = jnp.sum(recv_g[...], axis=0)

    def total_out(i, _):
        to = lax.rem(c + i, CHAN)

        @pl.when(jnp.logical_not(jnp.logical_and(is_self, i == 0)))
        def _():
            copy(send_t.at[0], recv_t.at[f], 6, own_part, to).start()

        return 0

    lax.fori_loop(0, CHAN, total_out, 0)

    @pl.when(is_self)
    def _():
        recv_t[f] = send_t[0]

    whole(recv_b, SEQ - 1, 4).wait_recv()
    tokens = nt(flip(LANES), recv_b[...].reshape(512, LANES)).astype(BF16)
    result = nn(tokens, route[...])
    for n in range(4):
        here = pl.ds(LANES * n, LANES)
        part = result[:, LANES * n : LANES * (n + 1)]
        inner_grad[here, :] = (part * va[here, :].astype(F32)).astype(BF16)
        value_grad[here, :] = (part * ig[here, :].astype(F32)).astype(BF16)

    @pl.when(is_self)
    def _():
        whole(recv_t, TAPS - 1, 6).wait()

    @pl.when(jnp.logical_not(is_self))
    def _():
        whole(recv_t, TAPS, 6).wait()

    scale = float(512 * SEQ * LANES * CHAN // TAPS) ** -0.5
    back = flip(LANES).astype(F32)
    for n in range(4):
        part = lax.dot_general(
            back, recv_t[:, n, :], (((1,), (1,)), ((), ())),
            precision=lax.Precision.HIGHEST, preferred_element_type=F32,
        )
        filter_grad[LANES * n : LANES * (n + 1), :] = part * scale

    whole(recv_h, SEQ - 1, 0).wait_send()
    for n, ref in ((1, recv_x), (2, recv_u), (3, recv_c), (4, recv_b), (5, recv_g)):
        whole(ref, SEQ - 1, n).wait_send()


def on_device(outer_gate, inner_gate, values, filters, cotangent):
    wide = jax.ShapeDtypeStruct((512, LANES), BF16)
    slots = pltpu.VMEM((SEQ, 16, LANES), BF16)
    vmem = pl.BlockSpec(memory_space=pltpu.VMEM)
    return pl.pallas_call(
        kernel,
        out_shape=(wide, wide, wide, wide, jax.ShapeDtypeStruct((512, TAPS), F32)),
        in_specs=[vmem] * 5,
        out_specs=(vmem,) * 5,
        scratch_shapes=[
            pltpu.VMEM((TAPS, 4, LANES), BF16),
            slots, slots, slots, slots,
            pltpu.VMEM((2 + SEQ, 4, LANES), F32),
            pltpu.VMEM((1, 4, LANES), F32),
            pltpu.VMEM((SEQ, 4, LANES), BF16),
            slots, slots, slots, slots,
            pltpu.VMEM((SEQ, 4, LANES), F32),
            pltpu.VMEM((TAPS, 4, LANES), F32),
            pltpu.VMEM((129 * LANES, LANES), BF16),
            pltpu.VMEM((2 * ROWS, 1024), BF16),
            pltpu.VMEM((ROWS + 64, 1024), BF16),
            pltpu.VMEM((ROWS, ROWS), BF16),
            pltpu.VMEM((ROWS, ROWS), F32),
            pltpu.VMEM((512, 512), BF16),
            pltpu.SemaphoreType.DMA((7,)),
            pltpu.SemaphoreType.DMA((7,)),
        ],
        compiler_params=pltpu.CompilerParams(
            collective_id=0, has_side_effects=True, vmem_limit_bytes=40 * 2**20
        ),
    )(outer_gate, inner_gate, values, filters, cotangent)


def solution(mesh):
    placed = (P("seq", "chan"),) * 3 + (P("seq", None), P("seq", "chan"))
    return jax.shard_map(
        on_device,
        mesh=mesh,
        in_specs=placed,
        out_specs=(P("seq", "chan"),) * 4 + (P("seq", None),),
        check_vma=False,
    )
```

```python
import functools

import jax
import jax.numpy as jnp
from jax import lax
from jax.experimental import pallas as pl
from jax.experimental.pallas import tpu as pltpu
from jax.sharding import PartitionSpec as P

BF16 = jnp.bfloat16
F32 = jnp.float32
MESH = pl.DeviceIdType.MESH
SEQ = 32
CHAN = 16
TAPS = 16
LANES = 128
ROWS = 256


def nn(a, b):
    return lax.dot_general(a, b, (((1,), (0,)), ((), ())), preferred_element_type=F32)


def nt(a, b):
    return lax.dot_general(a, b, (((1,), (1,)), ((), ())), preferred_element_type=F32)


def iota(shape, axis):
    return lax.broadcasted_iota(jnp.int32, shape, axis)


def one_hot(hit):
    return jnp.where(hit, 1.0, 0.0).astype(BF16)


def eye(n):
    return one_hot(iota((n, n), 0) == iota((n, n), 1))


def flip(n):
    return one_hot(iota((n, n), 0) + iota((n, n), 1) == n - 1)


def routing():
    row, col = iota((512, 512), 0), iota((512, 512), 1)
    s, p, b, k = row >> 4, (row >> 3) & 1, (row >> 2) & 1, row & 3
    wanted = (2 * b + 1 - p) * LANES + (s >> 1) + TAPS * (4 * (s & 1) + k)
    return one_hot(col == wanted)


def stack_tokens(x, order):
    return jnp.concatenate([x[LANES * n : LANES * (n + 1)] for n in order], axis=1)


def shear(x):
    return pltpu.roll(x, 0, 1, stride=1, stride_axis=0)


def upper():
    return iota((LANES, LANES), 1) >= iota((LANES, LANES), 0)


def toeplitz(taps, w):
    w[0:LANES, :] = jnp.zeros((LANES, LANES), BF16)
    keep = upper()

    def body(s, before):
        for n in range(4):
            h = taps[s, n : n + 1, :].astype(F32)
            now = shear(jnp.broadcast_to(h, (LANES, LANES)))
            at = pl.multiple_of((4 * s + n + 1) * LANES, LANES)
            w[pl.ds(at, LANES), :] = jnp.where(keep, now, before).astype(BF16)
            before = now
        return before

    lax.fori_loop(0, SEQ, body, jnp.zeros((LANES, LANES), F32), unroll=8)


def unpack(slots):
    wide = slots[...].astype(F32)
    return jnp.concatenate(
        [wide[:, 0:8].reshape(ROWS, LANES), wide[:, 8:16].reshape(ROWS, LANES)], axis=1
    )


def pack(y):
    return jnp.concatenate(
        [y[:, :LANES].reshape(SEQ, 8, LANES), y[:, LANES:].reshape(SEQ, 8, LANES)], axis=1
    ).astype(BF16)


def spread_x(x, xs):
    xs[0:ROWS, :] = jnp.zeros((ROWS, 1024), BF16)
    row = iota((ROWS, ROWS), 0)
    for d in range(4):
        moved = x if d == 0 else jnp.where(row >= 4 * d, pltpu.roll(x, 4 * d, 0), 0.0)
        xs[ROWS:, ROWS * d : ROWS * (d + 1)] = moved.astype(BF16)


def spread_u(u, us):
    us[ROWS:, :] = jnp.zeros((us.shape[0] - ROWS, 1024), BF16)
    row = iota((ROWS, ROWS), 0)
    for d in range(4):
        moved = u if d == 0 else jnp.where(row < ROWS - 4 * d, pltpu.roll(u, ROWS - 4 * d, 0), 0.0)
        us[0:ROWS, ROWS * d : ROWS * (d + 1)] = moved.astype(BF16)


def lag_weights(w, group):
    at = pl.multiple_of(group * 1024, 1024)
    return jnp.concatenate(
        [w[pl.ds(at, 1024), :], w[pl.ds(pl.multiple_of(at + LANES, LANES), 1024), :]], axis=1
    )


def convolve(xs, w, y):
    y[...] = jnp.zeros((ROWS, ROWS), F32)
    for quarter in range(4):
        size = ROWS - 64 * quarter

        def body(g, _):
            at = pl.multiple_of(ROWS - 16 * g, 16)
            y[64 * quarter :, :] += nn(xs[pl.ds(at, size), :], lag_weights(w, 4 * quarter + g))
            return 0

        lax.fori_loop(0, 4, body, 0, unroll=4)


def convolve_back(us, w, y):
    y[...] = jnp.zeros((ROWS, ROWS), F32)
    for quarter in range(4):
        size = ROWS - 64 * quarter

        def body(g, _):
            group = 4 * quarter + g
            at = pl.multiple_of(16 * group, 16)
            y[0:size, :] += nn(us[pl.ds(at, size), :], lag_weights(w, group))
            return 0

        lax.fori_loop(0, 4, body, 0, unroll=4)


def correlate(ut, xs, out):
    keep = upper()

    def emit(before, now, group, e):
        line = jnp.sum(jnp.where(keep, before, now), axis=0, keepdims=True)
        out[2 * group + (e + 6) // 4, (e + 6) % 4, :] = line[0]

    def body(group, carry):
        before, edge = carry
        at = pl.multiple_of(ROWS - 16 * group, 16)
        pairs = nn(ut[...], xs[pl.ds(at, ROWS), :])
        for e in range(8):
            low = pairs[0:LANES, LANES * e : LANES * (e + 1)]
            high = edge if e == 0 else pairs[LANES:, LANES * (e - 1) : LANES * e]
            now = shear(low + high)
            emit(before, now, group, e)
            before = now
        return before, pairs[LANES:, LANES * 7 :]

    zero = jnp.zeros((LANES, LANES), F32)
    before, edge = lax.fori_loop(0, 16, body, (zero, zero), unroll=16)
    now = shear(edge)
    emit(before, now, 16, 0)
    emit(now, zero, 16, 1)


def product(a, b):
    return a[...].astype(F32) * b[...].astype(F32)


def kernel(
    og_far, ig_far, va_far, taps_far, ct_far,
    sums, grads,
    send_h, send_x, send_u, send_c, send_b, send_g, send_t,
    recv_h, recv_x, recv_u, recv_c, recv_b, recv_g, recv_t,
    og, ig, va, taps, ct, w, xs, us, ut, y, route, sems_out, sems_in, fetched,
):
    s, c = lax.axis_index("seq"), lax.axis_index("chan")
    f, half = s // 2, s % 2
    own_part = 16 * half + c
    is_self = s == own_part

    def device(seq, chan):
        return {"seq": seq, "chan": chan}

    fetches = [
        pltpu.make_async_copy(far, near, fetched.at[n])
        for n, (far, near) in enumerate(
            ((taps_far, taps), (ig_far, ig), (va_far, va), (ct_far, ct), (og_far, og))
        )
    ]
    for fetch in fetches:
        fetch.start()

    barrier = pltpu.get_barrier_semaphore()

    def greet(seq, chan):
        pl.semaphore_signal(barrier, inc=1, device_id=device(seq, chan), device_id_type=MESH)

    def greet_seq(ahead, i, _):
        greet(lax.rem(s // 8 + i // 2, 4) * 8 + lax.rem(s // 2 + ahead, 4) * 2 + lax.rem(s + i, 2), c)
        return 0

    def greet_chan(i, _):
        greet(s, lax.rem(c + i, CHAN))
        greet(2 * f + 1 - half, lax.rem(c + i, CHAN))
        return 0

    def greet_source(i, _):
        @pl.when(jnp.logical_not(jnp.logical_and(is_self, i == f)))
        def _():
            greet(2 * i + s // 16, lax.rem(s, 16))

        return 0

    for ahead in (2, 1, 3, 0):
        lax.fori_loop(0 if ahead else 1, 8, functools.partial(greet_seq, ahead), 0)
    lax.fori_loop(1, CHAN, greet_chan, 0)
    greet(2 * f + 1 - half, c)
    lax.fori_loop(0, TAPS, greet_source, 0)

    route[...] = routing()
    fetches[0].wait()
    for n in range(4):
        send_h[:, n, :] = taps[:, LANES * n : LANES * (n + 1)]
    fetches[1].wait()
    fetches[2].wait()
    inner = stack_tokens(product(ig, va).astype(BF16), range(4))
    send_x[...] = nt(route[...], inner).astype(BF16).reshape(SEQ, 16, LANES)
    @pl.when(is_self)
    def _():
        pl.semaphore_wait(barrier, 2 * (SEQ - 1) + TAPS - 1)

    @pl.when(jnp.logical_not(is_self))
    def _():
        pl.semaphore_wait(barrier, 2 * (SEQ - 1) + TAPS)

    def copy(src, dst, n, seq, chan):
        return pltpu.make_async_remote_copy(
            src_ref=src, dst_ref=dst, send_sem=sems_out.at[n], recv_sem=sems_in.at[n],
            device_id=device(seq, chan), device_id_type=MESH,
        )

    y_at, z_at, core_at = s // 8, (s // 2) % 4, s % 2

    def exchange_part(src, dst, n, slot, steps):
        def body(i, _):
            for step in steps:
                ahead = lax.rem(z_at + step, 4) * 2 + lax.rem(core_at + i, 2)
                to = lax.rem(y_at + i // 2, 4) * 8 + ahead
                copy(src.at[slot(to)], dst.at[s], n, to, c).start()
            return 0

        lax.fori_loop(1 if steps == (0,) else 0, 8, body, 0)

    def exchange(src, dst, n, slot):
        for steps in ((2,), (1, 3), (0,)):
            exchange_part(src, dst, n, slot, steps)
        dst[s] = src[slot(s)]

    def whole(ref, count, n):
        part = ref.at[pl.ds(0, count)]
        return copy(part, part, n, s, c)

    def send_taps():
        exchange(send_h, recv_h, 0, lambda to: to // 2)

    def send_inner():
        exchange(send_x, recv_x, 1, lambda to: to)

    def send_upstream():
        fetches[3].wait()
        fetches[4].wait()
        upstream = stack_tokens(product(ct, og).astype(BF16), (1, 0, 3, 2))
        upstream = nn(flip(LANES), upstream).astype(BF16)
        send_u[...] = nt(route[...], upstream).astype(BF16).reshape(SEQ, 16, LANES)
        exchange(send_u, recv_u, 2, lambda to: to)

    def take_taps():
        whole(recv_h, SEQ - 1, 0).wait_recv()
        toeplitz(recv_h, w)

    def take_inner():
        whole(recv_x, SEQ - 1, 1).wait_recv()
        spread_x(unpack(recv_x), xs)

    def take_upstream():
        whole(recv_u, SEQ - 1, 2).wait_recv()
        u = unpack(recv_u)
        spread_u(u, us)
        ut[...] = nt(eye(ROWS), u.astype(BF16)).astype(BF16)

    def forward():
        convolve(xs, w, y)
        send_c[...] = pack(y[...])
        exchange(send_c, recv_c, 3, lambda to: to)

    def backward():
        convolve_back(us, w, y)
        send_b[...] = pack(y[...])

    def send_backward_far():
        exchange_part(send_b, recv_b, 4, lambda to: to, (2,))

    def send_backward_near():
        exchange_part(send_b, recv_b, 4, lambda to: to, (1, 3))
        exchange_part(send_b, recv_b, 4, lambda to: to, (0,))
        recv_b[s] = send_b[s]

    def correlation():
        correlate(ut, xs, send_g)

        def parts_out(i, _):
            to = lax.rem(c + i, CHAN)
            here = c * 2 + half

            @pl.when(i > 0)
            def _():
                copy(send_g.at[2 + 16 * half + to], recv_g.at[here], 5, s, to).start()

            other = 1 - half
            copy(send_g.at[2 + 16 * other + to], recv_g.at[here], 5, 2 * f + other, to).start()
            return 0

        lax.fori_loop(0, CHAN, parts_out, 0)
        recv_g[c * 2 + half] = send_g[2 + own_part]

    def totals():
        whole(recv_g, SEQ - 1, 5).wait_recv()
        send_t[0] = jnp.sum(recv_g[...], axis=0)

        def total_out(i, _):
            to = lax.rem(c + i, CHAN)

            @pl.when(jnp.logical_not(jnp.logical_and(is_self, i == 0)))
            def _():
                copy(send_t.at[0], recv_t.at[f], 6, own_part, to).start()

            return 0

        lax.fori_loop(0, CHAN, total_out, 0)

        @pl.when(is_self)
        def _():
            recv_t[f] = send_t[0]

    send_taps()
    send_inner()
    send_upstream()
    take_taps()
    take_inner()
    forward()
    take_upstream()
    correlation()
    backward()
    send_backward_far()
    totals()
    send_backward_near()

    whole(recv_c, SEQ - 1, 3).wait_recv()
    tokens = nt(eye(LANES), recv_c[...].reshape(512, LANES)).astype(BF16)
    result = nn(tokens, route[...])
    for n in range(4):
        sums[pl.ds(LANES * (n ^ 1), LANES), :] = result[:, LANES * n : LANES * (n + 1)].astype(BF16)

    whole(recv_b, SEQ - 1, 4).wait_recv()
    tokens = nt(flip(LANES), recv_b[...].reshape(512, LANES)).astype(BF16)
    result = nn(tokens, route[...])
    for n in range(4):
        sums[pl.ds(512 + LANES * n, LANES), :] = result[:, LANES * n : LANES * (n + 1)].astype(BF16)

    @pl.when(is_self)
    def _():
        whole(recv_t, TAPS - 1, 6).wait()

    @pl.when(jnp.logical_not(is_self))
    def _():
        whole(recv_t, TAPS, 6).wait()

    grads[...] = recv_t[...]
    whole(recv_h, SEQ - 1, 0).wait_send()
    for n, ref in ((1, recv_x), (2, recv_u), (3, recv_c), (4, recv_b), (5, recv_g)):
        whole(ref, SEQ - 1, n).wait_send()


def finish(sums, grads, og, ig, va, ct, layer_out, outer_grad, inner_grad, value_grad, filter_grad):
    convolved, backward = sums[0:512].astype(F32), sums[512:].astype(F32)
    layer_out[...] = (og[...].astype(F32) * convolved).astype(BF16)
    outer_grad[...] = (ct[...].astype(F32) * convolved).astype(BF16)
    inner_grad[...] = (backward * va[...].astype(F32)).astype(BF16)
    value_grad[...] = (backward * ig[...].astype(F32)).astype(BF16)
    scale = float(512 * SEQ * LANES * CHAN // TAPS) ** -0.5
    back = flip(LANES).astype(F32)
    for n in range(4):
        part = lax.dot_general(
            grads[:, n, :], back, (((1,), (0,)), ((), ())),
            precision=lax.Precision.HIGHEST, preferred_element_type=F32,
        )
        filter_grad[:, LANES * n : LANES * (n + 1)] = part * scale


def on_device(outer_gate, inner_gate, values, filters, cotangent):
    wide = jax.ShapeDtypeStruct((512, LANES), BF16)
    slots = pltpu.VMEM((SEQ, 16, LANES), BF16)
    near = pltpu.VMEM((512, LANES), BF16)
    vmem = pl.BlockSpec(memory_space=pltpu.VMEM)
    sums, grads = pl.pallas_call(
        kernel,
        out_shape=(
            jax.ShapeDtypeStruct((1024, LANES), BF16),
            jax.ShapeDtypeStruct((TAPS, 4, LANES), F32),
        ),
        in_specs=[pl.BlockSpec(memory_space=pltpu.HBM)] * 5,
        out_specs=(vmem,) * 2,
        scratch_shapes=[
            pltpu.VMEM((TAPS, 4, LANES), BF16),
            slots, slots, slots, slots,
            pltpu.VMEM((2 + SEQ, 4, LANES), F32),
            pltpu.VMEM((1, 4, LANES), F32),
            pltpu.VMEM((SEQ, 4, LANES), BF16),
            slots, slots, slots, slots,
            pltpu.VMEM((SEQ, 4, LANES), F32),
            pltpu.VMEM((TAPS, 4, LANES), F32),
            near, near, near,
            pltpu.VMEM((TAPS, 512), BF16),
            near,
            pltpu.VMEM((129 * LANES, LANES), BF16),
            pltpu.VMEM((2 * ROWS, 1024), BF16),
            pltpu.VMEM((ROWS + 64, 1024), BF16),
            pltpu.VMEM((ROWS, ROWS), BF16),
            pltpu.VMEM((ROWS, ROWS), F32),
            pltpu.VMEM((512, 512), BF16),
            pltpu.SemaphoreType.DMA((7,)),
            pltpu.SemaphoreType.DMA((7,)),
            pltpu.SemaphoreType.DMA((5,)),
        ],
        compiler_params=pltpu.CompilerParams(
            collective_id=0, has_side_effects=True, vmem_limit_bytes=62 * 2**20
        ),
    )(outer_gate, inner_gate, values, filters.T, cotangent)
    *wides, filter_grad = pl.pallas_call(
        finish,
        out_shape=(wide, wide, wide, wide, jax.ShapeDtypeStruct((TAPS, 512), F32)),
        in_specs=[vmem] * 6,
        out_specs=(vmem,) * 5,
    )(sums, grads, outer_gate, inner_gate, values, cotangent)
    return (*wides, filter_grad.T)


def solution(mesh):
    placed = (P("seq", "chan"),) * 3 + (P("seq", None), P("seq", "chan"))
    return jax.shard_map(
        on_device,
        mesh=mesh,
        in_specs=placed,
        out_specs=(P("seq", "chan"),) * 4 + (P("seq", None),),
        check_vma=False,
    )
```

```python
import functools

import jax
import jax.numpy as jnp
from jax import lax
from jax.experimental import pallas as pl
from jax.experimental.pallas import tpu as pltpu
from jax.sharding import PartitionSpec as P

BF16 = jnp.bfloat16
F32 = jnp.float32
MESH = pl.DeviceIdType.MESH
SEQ = 32
CHAN = 16
TAPS = 16
LANES = 128
ROWS = 256


def nn(a, b):
    return lax.dot_general(a, b, (((1,), (0,)), ((), ())), preferred_element_type=F32)


def nt(a, b):
    return lax.dot_general(a, b, (((1,), (1,)), ((), ())), preferred_element_type=F32)


def iota(shape, axis):
    return lax.broadcasted_iota(jnp.int32, shape, axis)


def one_hot(hit):
    return jnp.where(hit, 1.0, 0.0).astype(BF16)


def eye(n):
    return one_hot(iota((n, n), 0) == iota((n, n), 1))


def flip(n):
    return one_hot(iota((n, n), 0) + iota((n, n), 1) == n - 1)


def routing():
    row, col = iota((512, 512), 0), iota((512, 512), 1)
    s, p, b, k = row >> 4, (row >> 3) & 1, (row >> 2) & 1, row & 3
    wanted = (2 * b + 1 - p) * LANES + (s >> 1) + TAPS * (4 * (s & 1) + k)
    return one_hot(col == wanted)


def stack_tokens(x, order):
    return jnp.concatenate([x[LANES * n : LANES * (n + 1)] for n in order], axis=1)


def shear(x):
    return pltpu.roll(x, 0, 1, stride=1, stride_axis=0)


def upper():
    return iota((LANES, LANES), 1) >= iota((LANES, LANES), 0)


def toeplitz(taps, w):
    w[0:LANES, :] = jnp.zeros((LANES, LANES), BF16)
    keep = upper()

    def body(s, before):
        for n in range(4):
            h = taps[s, n : n + 1, :].astype(F32)
            now = shear(jnp.broadcast_to(h, (LANES, LANES)))
            at = pl.multiple_of((4 * s + n + 1) * LANES, LANES)
            w[pl.ds(at, LANES), :] = jnp.where(keep, now, before).astype(BF16)
            before = now
        return before

    lax.fori_loop(0, SEQ, body, jnp.zeros((LANES, LANES), F32), unroll=8)


def unpack(slots):
    wide = slots[...].astype(F32)
    return jnp.concatenate(
        [wide[:, 0:8].reshape(ROWS, LANES), wide[:, 8:16].reshape(ROWS, LANES)], axis=1
    )


def pack(y):
    return jnp.concatenate(
        [y[:, :LANES].reshape(SEQ, 8, LANES), y[:, LANES:].reshape(SEQ, 8, LANES)], axis=1
    ).astype(BF16)


def spread_x(x, xs):
    xs[0:ROWS, :] = jnp.zeros((ROWS, 1024), BF16)
    row = iota((ROWS, ROWS), 0)
    for d in range(4):
        moved = x if d == 0 else jnp.where(row >= 4 * d, pltpu.roll(x, 4 * d, 0), 0.0)
        xs[ROWS:, ROWS * d : ROWS * (d + 1)] = moved.astype(BF16)


def spread_u(u, us):
    us[ROWS:, :] = jnp.zeros((us.shape[0] - ROWS, 1024), BF16)
    row = iota((ROWS, ROWS), 0)
    for d in range(4):
        moved = u if d == 0 else jnp.where(row < ROWS - 4 * d, pltpu.roll(u, ROWS - 4 * d, 0), 0.0)
        us[0:ROWS, ROWS * d : ROWS * (d + 1)] = moved.astype(BF16)


def lag_weights(w, group):
    at = pl.multiple_of(group * 1024, 1024)
    return jnp.concatenate(
        [w[pl.ds(at, 1024), :], w[pl.ds(pl.multiple_of(at + LANES, LANES), 1024), :]], axis=1
    )


def convolve(xs, w, y):
    y[...] = jnp.zeros((ROWS, ROWS), F32)
    for quarter in range(4):
        size = ROWS - 64 * quarter

        def body(g, _):
            at = pl.multiple_of(ROWS - 16 * g, 16)
            y[64 * quarter :, :] += nn(xs[pl.ds(at, size), :], lag_weights(w, 4 * quarter + g))
            return 0

        lax.fori_loop(0, 4, body, 0, unroll=4)


def convolve_back(us, w, y):
    y[...] = jnp.zeros((ROWS, ROWS), F32)
    for quarter in range(4):
        size = ROWS - 64 * quarter

        def body(g, _):
            group = 4 * quarter + g
            at = pl.multiple_of(16 * group, 16)
            y[0:size, :] += nn(us[pl.ds(at, size), :], lag_weights(w, group))
            return 0

        lax.fori_loop(0, 4, body, 0, unroll=4)


def correlate(ut, xs, out):
    keep = upper()

    def emit(before, now, group, e):
        line = jnp.sum(jnp.where(keep, before, now), axis=0, keepdims=True)
        out[2 * group + (e + 6) // 4, (e + 6) % 4, :] = line[0]

    def body(group, carry):
        before, edge = carry
        at = pl.multiple_of(ROWS - 16 * group, 16)
        pairs = nn(ut[...], xs[pl.ds(at, ROWS), :])
        for e in range(8):
            low = pairs[0:LANES, LANES * e : LANES * (e + 1)]
            high = edge if e == 0 else pairs[LANES:, LANES * (e - 1) : LANES * e]
            now = shear(low + high)
            emit(before, now, group, e)
            before = now
        return before, pairs[LANES:, LANES * 7 :]

    zero = jnp.zeros((LANES, LANES), F32)
    before, edge = lax.fori_loop(0, 16, body, (zero, zero), unroll=16)
    now = shear(edge)
    emit(before, now, 16, 0)
    emit(now, zero, 16, 1)


def product(a, b):
    return a[...].astype(F32) * b[...].astype(F32)


def kernel(
    og_far, ig_far, va_far, taps_far, ct_far,
    sums, grads,
    send_h, send_x, send_u, send_c, send_b, send_g, send_t,
    recv_h, recv_x, recv_u, recv_c, recv_b, recv_g, recv_t,
    og, ig, va, taps, ct, w, xs, us, ut, y, route, sems_out, sems_in, fetched,
):
    s, c = lax.axis_index("seq"), lax.axis_index("chan")
    f, half = s // 2, s % 2
    own_part = 16 * half + c
    is_self = s == own_part

    def device(seq, chan):
        return {"seq": seq, "chan": chan}

    fetches = [
        pltpu.make_async_copy(far, near, fetched.at[n])
        for n, (far, near) in enumerate(
            ((taps_far, taps), (ig_far, ig), (va_far, va), (ct_far, ct), (og_far, og))
        )
    ]
    for fetch in fetches:
        fetch.start()

    barrier = pltpu.get_barrier_semaphore()

    def greet(seq, chan):
        pl.semaphore_signal(barrier, inc=1, device_id=device(seq, chan), device_id_type=MESH)

    def greet_seq(ahead, i, _):
        greet(lax.rem(s // 8 + i // 2, 4) * 8 + lax.rem(s // 2 + ahead, 4) * 2 + lax.rem(s + i, 2), c)
        return 0

    def greet_chan(i, _):
        greet(s, lax.rem(c + i, CHAN))
        greet(2 * f + 1 - half, lax.rem(c + i, CHAN))
        return 0

    def greet_source(i, _):
        @pl.when(jnp.logical_not(jnp.logical_and(is_self, i == f)))
        def _():
            greet(2 * i + s // 16, lax.rem(s, 16))

        return 0

    for ahead in (2, 1, 3, 0):
        lax.fori_loop(0 if ahead else 1, 8, functools.partial(greet_seq, ahead), 0, unroll=True)
    lax.fori_loop(1, CHAN, greet_chan, 0, unroll=True)
    greet(2 * f + 1 - half, c)
    lax.fori_loop(0, TAPS, greet_source, 0, unroll=True)

    route[...] = routing()
    fetches[0].wait()
    for n in range(4):
        send_h[:, n, :] = taps[:, LANES * n : LANES * (n + 1)]
    fetches[1].wait()
    fetches[2].wait()
    inner = stack_tokens(product(ig, va).astype(BF16), range(4))
    send_x[...] = nt(route[...], inner).astype(BF16).reshape(SEQ, 16, LANES)
    @pl.when(is_self)
    def _():
        pl.semaphore_wait(barrier, 2 * (SEQ - 1) + TAPS - 1)

    @pl.when(jnp.logical_not(is_self))
    def _():
        pl.semaphore_wait(barrier, 2 * (SEQ - 1) + TAPS)

    def copy(src, dst, n, seq, chan):
        return pltpu.make_async_remote_copy(
            src_ref=src, dst_ref=dst, send_sem=sems_out.at[n], recv_sem=sems_in.at[n],
            device_id=device(seq, chan), device_id_type=MESH,
        )

    y_at, z_at, core_at = s // 8, (s // 2) % 4, s % 2

    def exchange_part(src, dst, n, slot, steps):
        def body(i, _):
            for step in steps:
                ahead = lax.rem(z_at + step, 4) * 2 + lax.rem(core_at + i, 2)
                to = lax.rem(y_at + i // 2, 4) * 8 + ahead
                copy(src.at[slot(to)], dst.at[s], n, to, c).start()
            return 0

        lax.fori_loop(1 if steps == (0,) else 0, 8, body, 0, unroll=True)

    def exchange(src, dst, n, slot):
        for steps in ((2,), (1, 3), (0,)):
            exchange_part(src, dst, n, slot, steps)
        dst[s] = src[slot(s)]

    def whole(ref, count, n):
        part = ref.at[pl.ds(0, count)]
        return copy(part, part, n, s, c)

    def send_taps():
        exchange(send_h, recv_h, 0, lambda to: to // 2)

    def send_inner():
        exchange(send_x, recv_x, 1, lambda to: to)

    def send_upstream():
        fetches[3].wait()
        fetches[4].wait()
        upstream = stack_tokens(product(ct, og).astype(BF16), (1, 0, 3, 2))
        upstream = nn(flip(LANES), upstream).astype(BF16)
        send_u[...] = nt(route[...], upstream).astype(BF16).reshape(SEQ, 16, LANES)
        exchange(send_u, recv_u, 2, lambda to: to)

    def take_taps():
        whole(recv_h, SEQ - 1, 0).wait_recv()
        toeplitz(recv_h, w)

    def take_inner():
        whole(recv_x, SEQ - 1, 1).wait_recv()
        spread_x(unpack(recv_x), xs)

    def take_upstream():
        whole(recv_u, SEQ - 1, 2).wait_recv()
        u = unpack(recv_u)
        spread_u(u, us)
        ut[...] = nt(eye(ROWS), u.astype(BF16)).astype(BF16)

    def forward():
        convolve(xs, w, y)
        send_c[...] = pack(y[...])
        exchange(send_c, recv_c, 3, lambda to: to)

    def backward():
        convolve_back(us, w, y)
        send_b[...] = pack(y[...])

    def send_backward_far():
        exchange_part(send_b, recv_b, 4, lambda to: to, (2,))

    def send_backward_near():
        exchange_part(send_b, recv_b, 4, lambda to: to, (1, 3))
        exchange_part(send_b, recv_b, 4, lambda to: to, (0,))
        recv_b[s] = send_b[s]

    def correlation():
        correlate(ut, xs, send_g)

        def parts_out(i, _):
            to = lax.rem(c + i, CHAN)
            here = c * 2 + half

            @pl.when(i > 0)
            def _():
                copy(send_g.at[2 + 16 * half + to], recv_g.at[here], 5, s, to).start()

            other = 1 - half
            copy(send_g.at[2 + 16 * other + to], recv_g.at[here], 5, 2 * f + other, to).start()
            return 0

        lax.fori_loop(0, CHAN, parts_out, 0, unroll=True)
        recv_g[c * 2 + half] = send_g[2 + own_part]

    def totals():
        whole(recv_g, SEQ - 1, 5).wait_recv()
        send_t[0] = jnp.sum(recv_g[...], axis=0)

        def total_out(i, _):
            to = lax.rem(c + i, CHAN)

            @pl.when(jnp.logical_not(jnp.logical_and(is_self, i == 0)))
            def _():
                copy(send_t.at[0], recv_t.at[f], 6, own_part, to).start()

            return 0

        lax.fori_loop(0, CHAN, total_out, 0, unroll=True)

        @pl.when(is_self)
        def _():
            recv_t[f] = send_t[0]

    send_taps()
    send_inner()
    send_upstream()
    take_taps()
    take_inner()
    forward()
    take_upstream()
    correlation()
    backward()
    send_backward_far()
    totals()
    send_backward_near()

    whole(recv_c, SEQ - 1, 3).wait_recv()
    tokens = nt(eye(LANES), recv_c[...].reshape(512, LANES)).astype(BF16)
    result = nn(tokens, route[...])
    for n in range(4):
        sums[pl.ds(LANES * (n ^ 1), LANES), :] = result[:, LANES * n : LANES * (n + 1)].astype(BF16)

    whole(recv_b, SEQ - 1, 4).wait_recv()
    tokens = nt(flip(LANES), recv_b[...].reshape(512, LANES)).astype(BF16)
    result = nn(tokens, route[...])
    for n in range(4):
        sums[pl.ds(512 + LANES * n, LANES), :] = result[:, LANES * n : LANES * (n + 1)].astype(BF16)

    @pl.when(is_self)
    def _():
        whole(recv_t, TAPS - 1, 6).wait()

    @pl.when(jnp.logical_not(is_self))
    def _():
        whole(recv_t, TAPS, 6).wait()

    grads[...] = recv_t[...]
    whole(recv_h, SEQ - 1, 0).wait_send()
    for n, ref in ((1, recv_x), (2, recv_u), (3, recv_c), (4, recv_b), (5, recv_g)):
        whole(ref, SEQ - 1, n).wait_send()


def finish(sums, grads, og, ig, va, ct, layer_out, outer_grad, inner_grad, value_grad, filter_grad):
    convolved, backward = sums[0:512].astype(F32), sums[512:].astype(F32)
    layer_out[...] = (og[...].astype(F32) * convolved).astype(BF16)
    outer_grad[...] = (ct[...].astype(F32) * convolved).astype(BF16)
    inner_grad[...] = (backward * va[...].astype(F32)).astype(BF16)
    value_grad[...] = (backward * ig[...].astype(F32)).astype(BF16)
    scale = float(512 * SEQ * LANES * CHAN // TAPS) ** -0.5
    back = flip(LANES).astype(F32)
    for n in range(4):
        part = lax.dot_general(
            grads[:, n, :], back, (((1,), (0,)), ((), ())),
            precision=lax.Precision.HIGHEST, preferred_element_type=F32,
        )
        filter_grad[:, LANES * n : LANES * (n + 1)] = part * scale


def on_device(outer_gate, inner_gate, values, filters, cotangent):
    wide = jax.ShapeDtypeStruct((512, LANES), BF16)
    slots = pltpu.VMEM((SEQ, 16, LANES), BF16)
    near = pltpu.VMEM((512, LANES), BF16)
    vmem = pl.BlockSpec(memory_space=pltpu.VMEM)
    sums, grads = pl.pallas_call(
        kernel,
        out_shape=(
            jax.ShapeDtypeStruct((1024, LANES), BF16),
            jax.ShapeDtypeStruct((TAPS, 4, LANES), F32),
        ),
        in_specs=[pl.BlockSpec(memory_space=pltpu.HBM)] * 5,
        out_specs=(vmem,) * 2,
        scratch_shapes=[
            pltpu.VMEM((TAPS, 4, LANES), BF16),
            slots, slots, slots, slots,
            pltpu.VMEM((2 + SEQ, 4, LANES), F32),
            pltpu.VMEM((1, 4, LANES), F32),
            pltpu.VMEM((SEQ, 4, LANES), BF16),
            slots, slots, slots, slots,
            pltpu.VMEM((SEQ, 4, LANES), F32),
            pltpu.VMEM((TAPS, 4, LANES), F32),
            near, near, near,
            pltpu.VMEM((TAPS, 512), BF16),
            near,
            pltpu.VMEM((129 * LANES, LANES), BF16),
            pltpu.VMEM((2 * ROWS, 1024), BF16),
            pltpu.VMEM((ROWS + 64, 1024), BF16),
            pltpu.VMEM((ROWS, ROWS), BF16),
            pltpu.VMEM((ROWS, ROWS), F32),
            pltpu.VMEM((512, 512), BF16),
            pltpu.SemaphoreType.DMA((7,)),
            pltpu.SemaphoreType.DMA((7,)),
            pltpu.SemaphoreType.DMA((5,)),
        ],
        compiler_params=pltpu.CompilerParams(
            collective_id=0, has_side_effects=True, vmem_limit_bytes=62 * 2**20
        ),
    )(outer_gate, inner_gate, values, filters.T, cotangent)
    *wides, filter_grad = pl.pallas_call(
        finish,
        out_shape=(wide, wide, wide, wide, jax.ShapeDtypeStruct((TAPS, 512), F32)),
        in_specs=[vmem] * 6,
        out_specs=(vmem,) * 5,
    )(sums, grads, outer_gate, inner_gate, values, cotangent)
    return (*wides, filter_grad.T)


def solution(mesh):
    placed = (P("seq", "chan"),) * 3 + (P("seq", None), P("seq", "chan"))
    return jax.shard_map(
        on_device,
        mesh=mesh,
        in_specs=placed,
        out_specs=(P("seq", "chan"),) * 4 + (P("seq", None),),
        check_vma=False,
    )
```

```python
import functools

import jax
import jax.numpy as jnp
from jax import lax
from jax.experimental import pallas as pl
from jax.experimental.pallas import tpu as pltpu
from jax.sharding import PartitionSpec as P

BF16 = jnp.bfloat16
F32 = jnp.float32
MESH = pl.DeviceIdType.MESH
SEQ = 32
CHAN = 16
TAPS = 16
LANES = 128
ROWS = 256


def nn(a, b):
    return lax.dot_general(a, b, (((1,), (0,)), ((), ())), preferred_element_type=F32)


def nt(a, b):
    return lax.dot_general(a, b, (((1,), (1,)), ((), ())), preferred_element_type=F32)


def iota(shape, axis):
    return lax.broadcasted_iota(jnp.int32, shape, axis)


def one_hot(hit):
    return jnp.where(hit, 1.0, 0.0).astype(BF16)


def eye(n):
    return one_hot(iota((n, n), 0) == iota((n, n), 1))


def flip(n):
    return one_hot(iota((n, n), 0) + iota((n, n), 1) == n - 1)


def routing():
    row, col = iota((512, 512), 0), iota((512, 512), 1)
    s, p, b, k = row >> 4, (row >> 3) & 1, (row >> 2) & 1, row & 3
    wanted = (2 * b + 1 - p) * LANES + (s >> 1) + TAPS * (4 * (s & 1) + k)
    return one_hot(col == wanted)


def stack_tokens(x, order):
    return jnp.concatenate([x[LANES * n : LANES * (n + 1)] for n in order], axis=1)


def shear(x):
    return pltpu.roll(x, 0, 1, stride=1, stride_axis=0)


def upper():
    return iota((LANES, LANES), 1) >= iota((LANES, LANES), 0)


def toeplitz(taps, w):
    w[0:LANES, :] = jnp.zeros((LANES, LANES), BF16)
    keep = upper()

    def body(s, before):
        for n in range(4):
            h = taps[s % 2, s // 2, n : n + 1, :].astype(F32)
            now = shear(jnp.broadcast_to(h, (LANES, LANES)))
            at = pl.multiple_of((4 * s + n + 1) * LANES, LANES)
            w[pl.ds(at, LANES), :] = jnp.where(keep, now, before).astype(BF16)
            before = now
        return before

    lax.fori_loop(0, SEQ, body, jnp.zeros((LANES, LANES), F32), unroll=8)


def unpack(slots):
    wide = slots[...].astype(F32)
    return jnp.concatenate(
        [wide[:, 0:8].reshape(ROWS, LANES), wide[:, 8:16].reshape(ROWS, LANES)], axis=1
    )


def pack(y):
    return jnp.concatenate(
        [y[:, :LANES].reshape(SEQ, 8, LANES), y[:, LANES:].reshape(SEQ, 8, LANES)], axis=1
    ).astype(BF16)


def spread_x(x, xs):
    xs[0:ROWS, :] = jnp.zeros((ROWS, 1024), BF16)
    row = iota((ROWS, ROWS), 0)
    for d in range(4):
        moved = x if d == 0 else jnp.where(row >= 4 * d, pltpu.roll(x, 4 * d, 0), 0.0)
        xs[ROWS:, ROWS * d : ROWS * (d + 1)] = moved.astype(BF16)


def spread_u(u, us):
    us[ROWS:, :] = jnp.zeros((us.shape[0] - ROWS, 1024), BF16)
    row = iota((ROWS, ROWS), 0)
    for d in range(4):
        moved = u if d == 0 else jnp.where(row < ROWS - 4 * d, pltpu.roll(u, ROWS - 4 * d, 0), 0.0)
        us[0:ROWS, ROWS * d : ROWS * (d + 1)] = moved.astype(BF16)


def lag_weights(w, group):
    at = pl.multiple_of(group * 1024, 1024)
    return jnp.concatenate(
        [w[pl.ds(at, 1024), :], w[pl.ds(pl.multiple_of(at + LANES, LANES), 1024), :]], axis=1
    )


def convolve(xs, w, y):
    y[...] = jnp.zeros((ROWS, ROWS), F32)
    for quarter in range(4):
        size = ROWS - 64 * quarter

        def body(g, _):
            at = pl.multiple_of(ROWS - 16 * g, 16)
            y[64 * quarter :, :] += nn(xs[pl.ds(at, size), :], lag_weights(w, 4 * quarter + g))
            return 0

        lax.fori_loop(0, 4, body, 0, unroll=4)


def convolve_back(us, w, y):
    y[...] = jnp.zeros((ROWS, ROWS), F32)
    for quarter in range(4):
        size = ROWS - 64 * quarter

        def body(g, _):
            group = 4 * quarter + g
            at = pl.multiple_of(16 * group, 16)
            y[0:size, :] += nn(us[pl.ds(at, size), :], lag_weights(w, group))
            return 0

        lax.fori_loop(0, 4, body, 0, unroll=4)


def correlate(ut, xs, out):
    keep = upper()

    def emit(before, now, group, e):
        line = jnp.sum(jnp.where(keep, before, now), axis=0, keepdims=True)
        out[2 * group + (e + 6) // 4, (e + 6) % 4, :] = line[0]

    def body(group, carry):
        before, edge = carry
        at = pl.multiple_of(ROWS - 16 * group, 16)
        pairs = nn(ut[...], xs[pl.ds(at, ROWS), :])
        for e in range(8):
            low = pairs[0:LANES, LANES * e : LANES * (e + 1)]
            high = edge if e == 0 else pairs[LANES:, LANES * (e - 1) : LANES * e]
            now = shear(low + high)
            emit(before, now, group, e)
            before = now
        return before, pairs[LANES:, LANES * 7 :]

    zero = jnp.zeros((LANES, LANES), F32)
    before, edge = lax.fori_loop(0, 16, body, (zero, zero), unroll=16)
    now = shear(edge)
    emit(before, now, 16, 0)
    emit(now, zero, 16, 1)


def product(a, b):
    return a[...].astype(F32) * b[...].astype(F32)


def kernel(
    og_far, ig_far, va_far, taps_far, ct_far,
    sums, grads,
    send_h, send_x, send_u, send_c, send_b, send_g, send_t,
    recv_h, recv_x, recv_u, recv_c, recv_b, recv_g, recv_t,
    og, ig, va, taps, ct, w, xs, us, ut, y, route, sems_out, sems_in, fetched,
):
    s, c = lax.axis_index("seq"), lax.axis_index("chan")
    f, half = s // 2, s % 2
    own_part = 16 * half + c
    is_self = s == own_part

    def device(seq, chan):
        return {"seq": seq, "chan": chan}

    fetches = [
        pltpu.make_async_copy(far, near, fetched.at[n])
        for n, (far, near) in enumerate(
            ((taps_far, taps), (ig_far, ig), (va_far, va), (ct_far, ct), (og_far, og))
        )
    ]
    for fetch in fetches:
        fetch.start()

    barrier = pltpu.get_barrier_semaphore()

    def greet(seq, chan):
        pl.semaphore_signal(barrier, inc=1, device_id=device(seq, chan), device_id_type=MESH)

    def greet_seq(ahead, i, _):
        greet(lax.rem(s // 8 + i // 2, 4) * 8 + lax.rem(s // 2 + ahead, 4) * 2 + lax.rem(s + i, 2), c)
        return 0

    def greet_chan(i, _):
        greet(s, lax.rem(c + i, CHAN))
        greet(2 * f + 1 - half, lax.rem(c + i, CHAN))
        return 0

    def greet_source(i, _):
        @pl.when(jnp.logical_not(jnp.logical_and(is_self, i == f)))
        def _():
            greet(2 * i + s // 16, lax.rem(s, 16))

        return 0

    for ahead in (2, 1, 3, 0):
        lax.fori_loop(0 if ahead else 1, 8, functools.partial(greet_seq, ahead), 0, unroll=True)
    lax.fori_loop(1, CHAN, greet_chan, 0, unroll=True)
    greet(2 * f + 1 - half, c)
    lax.fori_loop(0, TAPS, greet_source, 0, unroll=True)

    route[...] = routing()
    fetches[0].wait()
    for n in range(4):
        send_h[:, n, :] = taps[:, LANES * n : LANES * (n + 1)]
    fetches[1].wait()
    fetches[2].wait()
    inner = stack_tokens(product(ig, va).astype(BF16), range(4))
    send_x[...] = nt(route[...], inner).astype(BF16).reshape(SEQ, 16, LANES)
    @pl.when(is_self)
    def _():
        pl.semaphore_wait(barrier, 2 * (SEQ - 1) + TAPS - 1)

    @pl.when(jnp.logical_not(is_self))
    def _():
        pl.semaphore_wait(barrier, 2 * (SEQ - 1) + TAPS)

    def copy(src, dst, n, seq, chan):
        return pltpu.make_async_remote_copy(
            src_ref=src, dst_ref=dst, send_sem=sems_out.at[n], recv_sem=sems_in.at[n],
            device_id=device(seq, chan), device_id_type=MESH,
        )

    y_at, z_at, core_at = s // 8, (s // 2) % 4, s % 2

    def exchange_part(src, dst, n, slot, steps):
        def body(i, _):
            for step in steps:
                ahead = lax.rem(z_at + step, 4) * 2 + lax.rem(core_at + i, 2)
                to = lax.rem(y_at + i // 2, 4) * 8 + ahead
                copy(src.at[slot(to)], dst.at[s], n, to, c).start()
            return 0

        lax.fori_loop(1 if steps == (0,) else 0, 8, body, 0, unroll=True)

    def exchange(src, dst, n, slot):
        for steps in ((2,), (1, 3), (0,)):
            exchange_part(src, dst, n, slot, steps)
        dst[s] = src[slot(s)]

    def whole(ref, count, n):
        part = ref.at[pl.ds(0, count)]
        return copy(part, part, n, s, c)

    def send_taps():
        for ahead in (2, 1, 3, 0):
            for y_step in range(4):
                if ahead or y_step:
                    chip = lax.rem(y_at + y_step, 4) * 4 + lax.rem(z_at + ahead, 4)
                    copy(send_h.at[chip], recv_h.at[half, f], 0, 2 * chip + half, c).start()
        recv_h[half, f] = send_h[f]

    def swap_taps():
        whole(recv_h.at[half], TAPS - 1, 0).wait_recv()
        return copy(recv_h.at[half], recv_h.at[half], 7, 2 * f + 1 - half, c)

    def send_inner():
        exchange(send_x, recv_x, 1, lambda to: to)

    def send_upstream():
        fetches[3].wait()
        fetches[4].wait()
        upstream = stack_tokens(product(ct, og).astype(BF16), (1, 0, 3, 2))
        upstream = nn(flip(LANES), upstream).astype(BF16)
        send_u[...] = nt(route[...], upstream).astype(BF16).reshape(SEQ, 16, LANES)
        exchange(send_u, recv_u, 2, lambda to: to)

    def take_taps():
        swap = swap_taps()
        swap.start()
        swap.wait()
        toeplitz(recv_h, w)

    def take_inner():
        whole(recv_x, SEQ - 1, 1).wait_recv()
        spread_x(unpack(recv_x), xs)

    def take_upstream():
        whole(recv_u, SEQ - 1, 2).wait_recv()
        u = unpack(recv_u)
        spread_u(u, us)
        ut[...] = nt(eye(ROWS), u.astype(BF16)).astype(BF16)

    def forward():
        convolve(xs, w, y)
        send_c[...] = pack(y[...])
        exchange(send_c, recv_c, 3, lambda to: to)

    def backward():
        convolve_back(us, w, y)
        send_b[...] = pack(y[...])

    def send_backward_far():
        exchange_part(send_b, recv_b, 4, lambda to: to, (2,))

    def send_backward_near():
        exchange_part(send_b, recv_b, 4, lambda to: to, (1, 3))
        exchange_part(send_b, recv_b, 4, lambda to: to, (0,))
        recv_b[s] = send_b[s]

    def correlation():
        correlate(ut, xs, send_g)

        def parts_out(i, _):
            to = lax.rem(c + i, CHAN)
            here = c * 2 + half

            @pl.when(i > 0)
            def _():
                copy(send_g.at[2 + 16 * half + to], recv_g.at[here], 5, s, to).start()

            other = 1 - half
            copy(send_g.at[2 + 16 * other + to], recv_g.at[here], 5, 2 * f + other, to).start()
            return 0

        lax.fori_loop(0, CHAN, parts_out, 0, unroll=True)
        recv_g[c * 2 + half] = send_g[2 + own_part]

    def totals():
        whole(recv_g, SEQ - 1, 5).wait_recv()
        send_t[0] = jnp.sum(recv_g[...], axis=0)

        def total_out(i, _):
            to = lax.rem(c + i, CHAN)

            @pl.when(jnp.logical_not(jnp.logical_and(is_self, i == 0)))
            def _():
                copy(send_t.at[0], recv_t.at[f], 6, own_part, to).start()

            return 0

        lax.fori_loop(0, CHAN, total_out, 0, unroll=True)

        @pl.when(is_self)
        def _():
            recv_t[f] = send_t[0]

    send_taps()
    send_inner()
    send_upstream()
    take_taps()
    take_inner()
    forward()
    take_upstream()
    correlation()
    backward()
    send_backward_far()
    totals()
    send_backward_near()

    whole(recv_c, SEQ - 1, 3).wait_recv()
    tokens = nt(eye(LANES), recv_c[...].reshape(512, LANES)).astype(BF16)
    result = nn(tokens, route[...])
    for n in range(4):
        sums[pl.ds(LANES * (n ^ 1), LANES), :] = result[:, LANES * n : LANES * (n + 1)].astype(BF16)

    whole(recv_b, SEQ - 1, 4).wait_recv()
    tokens = nt(flip(LANES), recv_b[...].reshape(512, LANES)).astype(BF16)
    result = nn(tokens, route[...])
    for n in range(4):
        sums[pl.ds(512 + LANES * n, LANES), :] = result[:, LANES * n : LANES * (n + 1)].astype(BF16)

    @pl.when(is_self)
    def _():
        whole(recv_t, TAPS - 1, 6).wait()

    @pl.when(jnp.logical_not(is_self))
    def _():
        whole(recv_t, TAPS, 6).wait()

    grads[...] = recv_t[...]
    whole(recv_h.at[half], TAPS - 1, 0).wait_send()
    for n, ref in ((1, recv_x), (2, recv_u), (3, recv_c), (4, recv_b), (5, recv_g)):
        whole(ref, SEQ - 1, n).wait_send()


def finish(sums, grads, og, ig, va, ct, layer_out, outer_grad, inner_grad, value_grad, filter_grad):
    convolved, backward = sums[0:512].astype(F32), sums[512:].astype(F32)
    layer_out[...] = (og[...].astype(F32) * convolved).astype(BF16)
    outer_grad[...] = (ct[...].astype(F32) * convolved).astype(BF16)
    inner_grad[...] = (backward * va[...].astype(F32)).astype(BF16)
    value_grad[...] = (backward * ig[...].astype(F32)).astype(BF16)
    scale = float(512 * SEQ * LANES * CHAN // TAPS) ** -0.5
    back = flip(LANES).astype(F32)
    for n in range(4):
        part = lax.dot_general(
            grads[:, n, :], back, (((1,), (0,)), ((), ())),
            precision=lax.Precision.HIGHEST, preferred_element_type=F32,
        )
        filter_grad[:, LANES * n : LANES * (n + 1)] = part * scale


def on_device(outer_gate, inner_gate, values, filters, cotangent):
    wide = jax.ShapeDtypeStruct((512, LANES), BF16)
    slots = pltpu.VMEM((SEQ, 16, LANES), BF16)
    near = pltpu.VMEM((512, LANES), BF16)
    vmem = pl.BlockSpec(memory_space=pltpu.VMEM)
    sums, grads = pl.pallas_call(
        kernel,
        out_shape=(
            jax.ShapeDtypeStruct((1024, LANES), BF16),
            jax.ShapeDtypeStruct((TAPS, 4, LANES), F32),
        ),
        in_specs=[pl.BlockSpec(memory_space=pltpu.HBM)] * 5,
        out_specs=(vmem,) * 2,
        scratch_shapes=[
            pltpu.VMEM((TAPS, 4, LANES), BF16),
            slots, slots, slots, slots,
            pltpu.VMEM((2 + SEQ, 4, LANES), F32),
            pltpu.VMEM((1, 4, LANES), F32),
            pltpu.VMEM((2, TAPS, 4, LANES), BF16),
            slots, slots, slots, slots,
            pltpu.VMEM((SEQ, 4, LANES), F32),
            pltpu.VMEM((TAPS, 4, LANES), F32),
            near, near, near,
            pltpu.VMEM((TAPS, 512), BF16),
            near,
            pltpu.VMEM((129 * LANES, LANES), BF16),
            pltpu.VMEM((2 * ROWS, 1024), BF16),
            pltpu.VMEM((ROWS + 64, 1024), BF16),
            pltpu.VMEM((ROWS, ROWS), BF16),
            pltpu.VMEM((ROWS, ROWS), F32),
            pltpu.VMEM((512, 512), BF16),
            pltpu.SemaphoreType.DMA((8,)),
            pltpu.SemaphoreType.DMA((8,)),
            pltpu.SemaphoreType.DMA((5,)),
        ],
        compiler_params=pltpu.CompilerParams(
            collective_id=0, has_side_effects=True, vmem_limit_bytes=62 * 2**20
        ),
    )(outer_gate, inner_gate, values, filters.T, cotangent)
    *wides, filter_grad = pl.pallas_call(
        finish,
        out_shape=(wide, wide, wide, wide, jax.ShapeDtypeStruct((TAPS, 512), F32)),
        in_specs=[vmem] * 6,
        out_specs=(vmem,) * 5,
    )(sums, grads, outer_gate, inner_gate, values, cotangent)
    return (*wides, filter_grad.T)


def solution(mesh):
    placed = (P("seq", "chan"),) * 3 + (P("seq", None), P("seq", "chan"))
    return jax.shard_map(
        on_device,
        mesh=mesh,
        in_specs=placed,
        out_specs=(P("seq", "chan"),) * 4 + (P("seq", None),),
        check_vma=False,
    )
```

```python
import functools

import jax
import jax.numpy as jnp
from jax import lax
from jax.experimental import pallas as pl
from jax.experimental.pallas import tpu as pltpu
from jax.sharding import PartitionSpec as P

BF16 = jnp.bfloat16
F32 = jnp.float32
MESH = pl.DeviceIdType.MESH
SEQ = 32
CHAN = 16
TAPS = 16
LANES = 128
ROWS = 256


def nn(a, b):
    return lax.dot_general(a, b, (((1,), (0,)), ((), ())), preferred_element_type=F32)


def nt(a, b):
    return lax.dot_general(a, b, (((1,), (1,)), ((), ())), preferred_element_type=F32)


def iota(shape, axis):
    return lax.broadcasted_iota(jnp.int32, shape, axis)


def one_hot(hit):
    return jnp.where(hit, 1.0, 0.0).astype(BF16)


def eye(n):
    return one_hot(iota((n, n), 0) == iota((n, n), 1))


def flip(n):
    return one_hot(iota((n, n), 0) + iota((n, n), 1) == n - 1)


def routing():
    row, col = iota((512, 512), 0), iota((512, 512), 1)
    s, p, b, k = row >> 4, (row >> 3) & 1, (row >> 2) & 1, row & 3
    wanted = (2 * b + 1 - p) * LANES + (s >> 1) + TAPS * (4 * (s & 1) + k)
    return one_hot(col == wanted)


def stack_tokens(x, order):
    return jnp.concatenate([x[LANES * n : LANES * (n + 1)] for n in order], axis=1)


def shear(x):
    return pltpu.roll(x, 0, 1, stride=1, stride_axis=0)


def upper():
    return iota((LANES, LANES), 1) >= iota((LANES, LANES), 0)


def toeplitz(taps, w):
    w[0:LANES, :] = jnp.zeros((LANES, LANES), BF16)
    keep = upper()

    def body(s, before):
        for n in range(4):
            h = taps[s % 2, s // 2, n : n + 1, :].astype(F32)
            now = shear(jnp.broadcast_to(h, (LANES, LANES)))
            at = pl.multiple_of((4 * s + n + 1) * LANES, LANES)
            w[pl.ds(at, LANES), :] = jnp.where(keep, now, before).astype(BF16)
            before = now
        return before

    lax.fori_loop(0, SEQ, body, jnp.zeros((LANES, LANES), F32), unroll=8)


def unpack(slots):
    wide = slots[...].astype(F32)
    return jnp.concatenate(
        [wide[:, 0:8].reshape(ROWS, LANES), wide[:, 8:16].reshape(ROWS, LANES)], axis=1
    )


def pack(y):
    return jnp.concatenate(
        [y[:, :LANES].reshape(SEQ, 8, LANES), y[:, LANES:].reshape(SEQ, 8, LANES)], axis=1
    ).astype(BF16)


def spread_x(x, xs):
    xs[0:ROWS, :] = jnp.zeros((ROWS, 1024), BF16)
    row = iota((ROWS, ROWS), 0)
    for d in range(4):
        moved = x if d == 0 else jnp.where(row >= 4 * d, pltpu.roll(x, 4 * d, 0), 0.0)
        xs[ROWS:, ROWS * d : ROWS * (d + 1)] = moved.astype(BF16)


def spread_u(u, us):
    us[ROWS:, :] = jnp.zeros((us.shape[0] - ROWS, 1024), BF16)
    row = iota((ROWS, ROWS), 0)
    for d in range(4):
        moved = u if d == 0 else jnp.where(row < ROWS - 4 * d, pltpu.roll(u, ROWS - 4 * d, 0), 0.0)
        us[0:ROWS, ROWS * d : ROWS * (d + 1)] = moved.astype(BF16)


def lag_weights(w, group):
    at = pl.multiple_of(group * 1024, 1024)
    return jnp.concatenate(
        [w[pl.ds(at, 1024), :], w[pl.ds(pl.multiple_of(at + LANES, LANES), 1024), :]], axis=1
    )


def convolve(xs, w, y):
    y[...] = jnp.zeros((ROWS, ROWS), F32)
    for quarter in range(4):
        size = ROWS - 64 * quarter

        def body(g, _):
            at = pl.multiple_of(ROWS - 16 * g, 16)
            y[64 * quarter :, :] += nn(xs[pl.ds(at, size), :], lag_weights(w, 4 * quarter + g))
            return 0

        lax.fori_loop(0, 4, body, 0, unroll=4)


def convolve_back(us, w, y):
    y[...] = jnp.zeros((ROWS, ROWS), F32)
    for quarter in range(4):
        size = ROWS - 64 * quarter

        def body(g, _):
            group = 4 * quarter + g
            at = pl.multiple_of(16 * group, 16)
            y[0:size, :] += nn(us[pl.ds(at, size), :], lag_weights(w, group))
            return 0

        lax.fori_loop(0, 4, body, 0, unroll=4)


def correlate(ut, xs, out):
    keep = upper()

    def emit(before, now, group, e):
        line = jnp.sum(jnp.where(keep, before, now), axis=0, keepdims=True)
        out[2 * group + (e + 6) // 4, (e + 6) % 4, :] = line[0]

    def body(group, carry):
        before, edge = carry
        at = pl.multiple_of(ROWS - 16 * group, 16)
        pairs = nn(ut[...], xs[pl.ds(at, ROWS), :])
        for e in range(8):
            low = pairs[0:LANES, LANES * e : LANES * (e + 1)]
            high = edge if e == 0 else pairs[LANES:, LANES * (e - 1) : LANES * e]
            now = shear(low + high)
            emit(before, now, group, e)
            before = now
        return before, pairs[LANES:, LANES * 7 :]

    zero = jnp.zeros((LANES, LANES), F32)
    before, edge = lax.fori_loop(0, 16, body, (zero, zero), unroll=16)
    now = shear(edge)
    emit(before, now, 16, 0)
    emit(now, zero, 16, 1)


def product(a, b):
    return a[...].astype(F32) * b[...].astype(F32)


def kernel(
    og_far, ig_far, va_far, taps_far, ct_far,
    sums, grads,
    send_h, send_x, send_u, send_c, send_b, send_g, send_t,
    recv_h, recv_x, recv_u, recv_c, recv_b, recv_g, recv_t,
    og, ig, va, taps, ct, w, xs, us, ut, y, route, sems_out, sems_in, fetched,
):
    s, c = lax.axis_index("seq"), lax.axis_index("chan")
    f, half = s // 2, s % 2
    own_part = 16 * half + c
    is_self = s == own_part

    def device(seq, chan):
        return {"seq": seq, "chan": chan}

    fetches = [
        pltpu.make_async_copy(far, near, fetched.at[n])
        for n, (far, near) in enumerate(
            ((taps_far, taps), (ig_far, ig), (va_far, va), (ct_far, ct), (og_far, og))
        )
    ]
    for fetch in fetches:
        fetch.start()

    barrier = pltpu.get_barrier_semaphore()

    def greet(seq, chan):
        pl.semaphore_signal(barrier, inc=1, device_id=device(seq, chan), device_id_type=MESH)

    def greet_seq(ahead, i, _):
        greet(lax.rem(s // 8 + i // 2, 4) * 8 + lax.rem(s // 2 + ahead, 4) * 2 + lax.rem(s + i, 2), c)
        return 0

    def greet_chan(i, _):
        greet(s, lax.rem(c + i, CHAN))
        greet(2 * f + 1 - half, lax.rem(c + i, CHAN))
        return 0

    def greet_source(i, _):
        @pl.when(jnp.logical_not(jnp.logical_and(is_self, i == f)))
        def _():
            greet(2 * i + s // 16, lax.rem(s, 16))

        return 0

    for ahead in (2, 1, 3, 0):
        lax.fori_loop(0 if ahead else 1, 8, functools.partial(greet_seq, ahead), 0, unroll=True)
    lax.fori_loop(1, CHAN, greet_chan, 0, unroll=True)
    greet(2 * f + 1 - half, c)
    lax.fori_loop(0, TAPS, greet_source, 0, unroll=True)

    route[...] = routing()
    fetches[0].wait()
    for n in range(4):
        send_h[:, n, :] = taps[:, LANES * n : LANES * (n + 1)]
    fetches[1].wait()
    fetches[2].wait()
    inner = stack_tokens(product(ig, va).astype(BF16), range(4))
    send_x[...] = nt(route[...], inner).astype(BF16).reshape(SEQ, 16, LANES)
    @pl.when(is_self)
    def _():
        pl.semaphore_wait(barrier, 2 * (SEQ - 1) + TAPS - 1)

    @pl.when(jnp.logical_not(is_self))
    def _():
        pl.semaphore_wait(barrier, 2 * (SEQ - 1) + TAPS)

    def copy(src, dst, n, seq, chan):
        return pltpu.make_async_remote_copy(
            src_ref=src, dst_ref=dst, send_sem=sems_out.at[n], recv_sem=sems_in.at[n],
            device_id=device(seq, chan), device_id_type=MESH,
        )

    y_at, z_at, core_at = s // 8, (s // 2) % 4, s % 2

    def exchange_part(src, dst, n, slot, steps):
        def body(i, _):
            for step in steps:
                ahead = lax.rem(z_at + step, 4) * 2 + lax.rem(core_at + i, 2)
                to = lax.rem(y_at + i // 2, 4) * 8 + ahead
                copy(src.at[slot(to)], dst.at[s], n, to, c).start()
            return 0

        lax.fori_loop(1 if steps == (0,) else 0, 8, body, 0, unroll=True)

    def exchange(src, dst, n, slot):
        for steps in ((2,), (1, 3), (0,)):
            exchange_part(src, dst, n, slot, steps)
        dst[s] = src[slot(s)]

    def whole(ref, count, n):
        part = ref.at[pl.ds(0, count)]
        return copy(part, part, n, s, c)

    def send_taps():
        for ahead in (2, 1, 3, 0):
            for y_step in range(4):
                if ahead or y_step:
                    chip = lax.rem(y_at + y_step, 4) * 4 + lax.rem(z_at + ahead, 4)
                    copy(send_h.at[chip], recv_h.at[half, f], 0, 2 * chip + half, c).start()
        recv_h[half, f] = send_h[f]

    def swap_taps():
        whole(recv_h.at[half], TAPS - 1, 0).wait_recv()
        return copy(recv_h.at[half], recv_h.at[half], 7, 2 * f + 1 - half, c)

    def send_inner():
        exchange(send_x, recv_x, 1, lambda to: to)

    def send_upstream():
        fetches[3].wait()
        fetches[4].wait()
        upstream = stack_tokens(product(ct, og).astype(BF16), (1, 0, 3, 2))
        upstream = nn(flip(LANES), upstream).astype(BF16)
        send_u[...] = nt(route[...], upstream).astype(BF16).reshape(SEQ, 16, LANES)
        exchange_part(send_u, recv_u, 2, lambda to: to, (2,))
        swap = swap_taps()
        swap.start()
        exchange_part(send_u, recv_u, 2, lambda to: to, (1, 3))
        exchange_part(send_u, recv_u, 2, lambda to: to, (0,))
        recv_u[s] = send_u[s]
        return swap

    def take_taps(swap):
        swap.wait()
        toeplitz(recv_h, w)

    def take_inner():
        whole(recv_x, SEQ - 1, 1).wait_recv()
        spread_x(unpack(recv_x), xs)

    def take_upstream():
        whole(recv_u, SEQ - 1, 2).wait_recv()
        ut[...] = nt(eye(ROWS), unpack(recv_u).astype(BF16)).astype(BF16)

    def forward():
        convolve(xs, w, y)
        send_c[...] = pack(y[...])
        exchange(send_c, recv_c, 3, lambda to: to)

    def backward():
        spread_u(unpack(recv_u), us)
        convolve_back(us, w, y)
        send_b[...] = pack(y[...])

    def send_backward_far():
        exchange_part(send_b, recv_b, 4, lambda to: to, (2,))

    def send_backward_near():
        exchange_part(send_b, recv_b, 4, lambda to: to, (1, 3))
        exchange_part(send_b, recv_b, 4, lambda to: to, (0,))
        recv_b[s] = send_b[s]

    def correlation():
        correlate(ut, xs, send_g)

        def parts_out(i, _):
            to = lax.rem(c + i, CHAN)
            here = c * 2 + half

            @pl.when(i > 0)
            def _():
                copy(send_g.at[2 + 16 * half + to], recv_g.at[here], 5, s, to).start()

            other = 1 - half
            copy(send_g.at[2 + 16 * other + to], recv_g.at[here], 5, 2 * f + other, to).start()
            return 0

        lax.fori_loop(0, CHAN, parts_out, 0, unroll=True)
        recv_g[c * 2 + half] = send_g[2 + own_part]

    def totals():
        whole(recv_g, SEQ - 1, 5).wait_recv()
        send_t[0] = jnp.sum(recv_g[...], axis=0).astype(BF16)

        def total_out(i, _):
            to = lax.rem(c + i, CHAN)

            @pl.when(jnp.logical_not(jnp.logical_and(is_self, i == 0)))
            def _():
                copy(send_t.at[0], recv_t.at[f], 6, own_part, to).start()

            return 0

        lax.fori_loop(0, CHAN, total_out, 0, unroll=True)

        @pl.when(is_self)
        def _():
            recv_t[f] = send_t[0]

    send_taps()
    send_inner()
    swap = send_upstream()
    take_taps(swap)
    take_inner()
    forward()
    take_upstream()
    correlation()
    backward()
    send_backward_far()
    totals()
    send_backward_near()

    whole(recv_c, SEQ - 1, 3).wait_recv()
    tokens = nt(eye(LANES), recv_c[...].reshape(512, LANES)).astype(BF16)
    result = nn(tokens, route[...])
    for n in range(4):
        sums[pl.ds(LANES * (n ^ 1), LANES), :] = result[:, LANES * n : LANES * (n + 1)].astype(BF16)

    whole(recv_b, SEQ - 1, 4).wait_recv()
    tokens = nt(flip(LANES), recv_b[...].reshape(512, LANES)).astype(BF16)
    result = nn(tokens, route[...])
    for n in range(4):
        sums[pl.ds(512 + LANES * n, LANES), :] = result[:, LANES * n : LANES * (n + 1)].astype(BF16)

    @pl.when(is_self)
    def _():
        whole(recv_t, TAPS - 1, 6).wait()

    @pl.when(jnp.logical_not(is_self))
    def _():
        whole(recv_t, TAPS, 6).wait()

    grads[...] = recv_t[...]
    whole(recv_h.at[half], TAPS - 1, 0).wait_send()
    for n, ref in ((1, recv_x), (2, recv_u), (3, recv_c), (4, recv_b), (5, recv_g)):
        whole(ref, SEQ - 1, n).wait_send()


def finish(sums, grads, og, ig, va, ct, layer_out, outer_grad, inner_grad, value_grad, filter_grad):
    convolved, backward = sums[0:512].astype(F32), sums[512:].astype(F32)
    layer_out[...] = (og[...].astype(F32) * convolved).astype(BF16)
    outer_grad[...] = (ct[...].astype(F32) * convolved).astype(BF16)
    inner_grad[...] = (backward * va[...].astype(F32)).astype(BF16)
    value_grad[...] = (backward * ig[...].astype(F32)).astype(BF16)
    scale = float(512 * SEQ * LANES * CHAN // TAPS) ** -0.5
    for n in range(4):
        part = nn(grads[:, n, :], flip(LANES))
        filter_grad[:, LANES * n : LANES * (n + 1)] = part * scale


def on_device(outer_gate, inner_gate, values, filters, cotangent):
    wide = jax.ShapeDtypeStruct((512, LANES), BF16)
    slots = pltpu.VMEM((SEQ, 16, LANES), BF16)
    near = pltpu.VMEM((512, LANES), BF16)
    vmem = pl.BlockSpec(memory_space=pltpu.VMEM)
    sums, grads = pl.pallas_call(
        kernel,
        out_shape=(
            jax.ShapeDtypeStruct((1024, LANES), BF16),
            jax.ShapeDtypeStruct((TAPS, 4, LANES), BF16),
        ),
        in_specs=[pl.BlockSpec(memory_space=pltpu.HBM)] * 5,
        out_specs=(vmem,) * 2,
        scratch_shapes=[
            pltpu.VMEM((TAPS, 4, LANES), BF16),
            slots, slots, slots, slots,
            pltpu.VMEM((2 + SEQ, 4, LANES), F32),
            pltpu.VMEM((1, 4, LANES), BF16),
            pltpu.VMEM((2, TAPS, 4, LANES), BF16),
            slots, slots, slots, slots,
            pltpu.VMEM((SEQ, 4, LANES), F32),
            pltpu.VMEM((TAPS, 4, LANES), BF16),
            near, near, near,
            pltpu.VMEM((TAPS, 512), BF16),
            near,
            pltpu.VMEM((129 * LANES, LANES), BF16),
            pltpu.VMEM((2 * ROWS, 1024), BF16),
            pltpu.VMEM((ROWS + 64, 1024), BF16),
            pltpu.VMEM((ROWS, ROWS), BF16),
            pltpu.VMEM((ROWS, ROWS), F32),
            pltpu.VMEM((512, 512), BF16),
            pltpu.SemaphoreType.DMA((8,)),
            pltpu.SemaphoreType.DMA((8,)),
            pltpu.SemaphoreType.DMA((5,)),
        ],
        compiler_params=pltpu.CompilerParams(
            collective_id=0, has_side_effects=True, vmem_limit_bytes=62 * 2**20
        ),
    )(outer_gate, inner_gate, values, filters.T, cotangent)
    *wides, filter_grad = pl.pallas_call(
        finish,
        out_shape=(wide, wide, wide, wide, jax.ShapeDtypeStruct((TAPS, 512), F32)),
        in_specs=[vmem] * 6,
        out_specs=(vmem,) * 5,
    )(sums, grads, outer_gate, inner_gate, values, cotangent)
    return (*wides, filter_grad.T)


def solution(mesh):
    placed = (P("seq", "chan"),) * 3 + (P("seq", None), P("seq", "chan"))
    return jax.shard_map(
        on_device,
        mesh=mesh,
        in_specs=placed,
        out_specs=(P("seq", "chan"),) * 4 + (P("seq", None),),
        check_vma=False,
    )
```

```python
import functools

import jax
import jax.numpy as jnp
from jax import lax
from jax.experimental import pallas as pl
from jax.experimental.pallas import tpu as pltpu
from jax.sharding import PartitionSpec as P

BF16 = jnp.bfloat16
F32 = jnp.float32
MESH = pl.DeviceIdType.MESH
SEQ = 32
CHAN = 16
TAPS = 16
LANES = 128
ROWS = 256


def nn(a, b):
    return lax.dot_general(a, b, (((1,), (0,)), ((), ())), preferred_element_type=F32)


def nt(a, b):
    return lax.dot_general(a, b, (((1,), (1,)), ((), ())), preferred_element_type=F32)


def iota(shape, axis):
    return lax.broadcasted_iota(jnp.int32, shape, axis)


def one_hot(hit):
    return jnp.where(hit, 1.0, 0.0).astype(BF16)


def eye(n):
    return one_hot(iota((n, n), 0) == iota((n, n), 1))


def flip(n):
    return one_hot(iota((n, n), 0) + iota((n, n), 1) == n - 1)


def routing():
    row, col = iota((512, 512), 0), iota((512, 512), 1)
    s, p, b, k = row >> 4, (row >> 3) & 1, (row >> 2) & 1, row & 3
    wanted = (2 * b + 1 - p) * LANES + (s >> 1) + TAPS * (4 * (s & 1) + k)
    return one_hot(col == wanted)


def stack_tokens(x, order):
    return jnp.concatenate([x[LANES * n : LANES * (n + 1)] for n in order], axis=1)


def shear(x):
    return pltpu.roll(x, 0, 1, stride=1, stride_axis=0)


def upper():
    return iota((LANES, LANES), 1) >= iota((LANES, LANES), 0)


def toeplitz(taps, w):
    w[0:LANES, :] = jnp.zeros((LANES, LANES), BF16)
    keep = upper()

    def body(s, before):
        for n in range(4):
            h = taps[s % 2, s // 2, n : n + 1, :].astype(F32)
            now = shear(jnp.broadcast_to(h, (LANES, LANES)))
            at = pl.multiple_of((4 * s + n + 1) * LANES, LANES)
            w[pl.ds(at, LANES), :] = jnp.where(keep, now, before).astype(BF16)
            before = now
        return before

    lax.fori_loop(0, SEQ, body, jnp.zeros((LANES, LANES), F32), unroll=16)


def unpack(slots):
    wide = slots[...].astype(F32)
    return jnp.concatenate(
        [wide[:, 0:8].reshape(ROWS, LANES), wide[:, 8:16].reshape(ROWS, LANES)], axis=1
    )


def pack(y):
    return jnp.concatenate(
        [y[:, :LANES].reshape(SEQ, 8, LANES), y[:, LANES:].reshape(SEQ, 8, LANES)], axis=1
    ).astype(BF16)


def spread_x(x, xs):
    xs[0:ROWS, :] = jnp.zeros((ROWS, 1024), BF16)
    row = iota((ROWS, ROWS), 0)
    for d in range(4):
        moved = x if d == 0 else jnp.where(row >= 4 * d, pltpu.roll(x, 4 * d, 0), 0.0)
        xs[ROWS:, ROWS * d : ROWS * (d + 1)] = moved.astype(BF16)


def spread_u(u, us):
    us[ROWS:, :] = jnp.zeros((us.shape[0] - ROWS, 1024), BF16)
    row = iota((ROWS, ROWS), 0)
    for d in range(4):
        moved = u if d == 0 else jnp.where(row < ROWS - 4 * d, pltpu.roll(u, ROWS - 4 * d, 0), 0.0)
        us[0:ROWS, ROWS * d : ROWS * (d + 1)] = moved.astype(BF16)


def lag_weights(w, group):
    at = pl.multiple_of(group * 1024, 1024)
    return jnp.concatenate(
        [w[pl.ds(at, 1024), :], w[pl.ds(pl.multiple_of(at + LANES, LANES), 1024), :]], axis=1
    )


def convolve(xs, w, y):
    y[...] = jnp.zeros((ROWS, ROWS), F32)
    for quarter in range(4):
        size = ROWS - 64 * quarter

        def body(g, _):
            at = pl.multiple_of(ROWS - 16 * g, 16)
            y[64 * quarter :, :] += nn(xs[pl.ds(at, size), :], lag_weights(w, 4 * quarter + g))
            return 0

        lax.fori_loop(0, 4, body, 0, unroll=4)


def convolve_back(us, w, y):
    y[...] = jnp.zeros((ROWS, ROWS), F32)
    for quarter in range(4):
        size = ROWS - 64 * quarter

        def body(g, _):
            group = 4 * quarter + g
            at = pl.multiple_of(16 * group, 16)
            y[0:size, :] += nn(us[pl.ds(at, size), :], lag_weights(w, group))
            return 0

        lax.fori_loop(0, 4, body, 0, unroll=4)


def correlate(ut, xs, out):
    keep = upper()

    def emit(before, now, group, e):
        line = jnp.sum(jnp.where(keep, before, now), axis=0, keepdims=True)
        out[2 * group + (e + 6) // 4, (e + 6) % 4, :] = line[0]

    def body(group, carry):
        before, edge = carry
        at = pl.multiple_of(ROWS - 16 * group, 16)
        pairs = nn(ut[...], xs[pl.ds(at, ROWS), :])
        for e in range(8):
            low = pairs[0:LANES, LANES * e : LANES * (e + 1)]
            high = edge if e == 0 else pairs[LANES:, LANES * (e - 1) : LANES * e]
            now = shear(low + high)
            emit(before, now, group, e)
            before = now
        return before, pairs[LANES:, LANES * 7 :]

    zero = jnp.zeros((LANES, LANES), F32)
    before, edge = lax.fori_loop(0, 16, body, (zero, zero), unroll=16)
    now = shear(edge)
    emit(before, now, 16, 0)
    emit(now, zero, 16, 1)


def product(a, b):
    return a[...].astype(F32) * b[...].astype(F32)


def kernel(
    og_far, ig_far, va_far, taps_far, ct_far,
    sums, grads,
    send_h, send_x, send_u, send_c, send_b, send_g, send_t,
    recv_h, recv_x, recv_u, recv_c, recv_b, recv_g, recv_t,
    og, ig, va, taps, ct, w, xs, us, ut, y, route, sems_out, sems_in, fetched,
):
    s, c = lax.axis_index("seq"), lax.axis_index("chan")
    f, half = s // 2, s % 2
    own_part = 16 * half + c
    is_self = s == own_part

    def device(seq, chan):
        return {"seq": seq, "chan": chan}

    fetches = [
        pltpu.make_async_copy(far, near, fetched.at[n])
        for n, (far, near) in enumerate(
            ((taps_far, taps), (ig_far, ig), (va_far, va), (ct_far, ct), (og_far, og))
        )
    ]
    for fetch in fetches:
        fetch.start()

    barrier = pltpu.get_barrier_semaphore()

    def greet(seq, chan):
        pl.semaphore_signal(barrier, inc=1, device_id=device(seq, chan), device_id_type=MESH)

    def greet_seq(ahead, i, _):
        greet(lax.rem(s // 8 + i // 2, 4) * 8 + lax.rem(s // 2 + ahead, 4) * 2 + lax.rem(s + i, 2), c)
        return 0

    def greet_chan(i, _):
        greet(s, lax.rem(c + i, CHAN))
        greet(2 * f + 1 - half, lax.rem(c + i, CHAN))
        return 0

    def greet_source(i, _):
        @pl.when(jnp.logical_not(jnp.logical_and(is_self, i == f)))
        def _():
            greet(2 * i + s // 16, lax.rem(s, 16))

        return 0

    for ahead in (2, 1, 3, 0):
        lax.fori_loop(0 if ahead else 1, 8, functools.partial(greet_seq, ahead), 0, unroll=True)
    lax.fori_loop(1, CHAN, greet_chan, 0, unroll=True)
    greet(2 * f + 1 - half, c)
    lax.fori_loop(0, TAPS, greet_source, 0, unroll=True)

    route[...] = routing()
    fetches[0].wait()
    for n in range(4):
        send_h[:, n, :] = taps[:, LANES * n : LANES * (n + 1)]
    fetches[1].wait()
    fetches[2].wait()
    inner = stack_tokens(product(ig, va).astype(BF16), range(4))
    send_x[...] = nt(route[...], inner).astype(BF16).reshape(SEQ, 16, LANES)
    fetches[3].wait()
    fetches[4].wait()
    upstream = stack_tokens(product(ct, og).astype(BF16), (1, 0, 3, 2))
    upstream = nn(flip(LANES), upstream).astype(BF16)
    send_u[...] = nt(route[...], upstream).astype(BF16).reshape(SEQ, 16, LANES)

    @pl.when(is_self)
    def _():
        pl.semaphore_wait(barrier, 2 * (SEQ - 1) + TAPS - 1)

    @pl.when(jnp.logical_not(is_self))
    def _():
        pl.semaphore_wait(barrier, 2 * (SEQ - 1) + TAPS)

    def copy(src, dst, n, seq, chan):
        return pltpu.make_async_remote_copy(
            src_ref=src, dst_ref=dst, send_sem=sems_out.at[n], recv_sem=sems_in.at[n],
            device_id=device(seq, chan), device_id_type=MESH,
        )

    y_at, z_at, core_at = s // 8, (s // 2) % 4, s % 2

    def exchange_part(src, dst, n, slot, steps):
        def body(i, _):
            for step in steps:
                ahead = lax.rem(z_at + step, 4) * 2 + lax.rem(core_at + i, 2)
                to = lax.rem(y_at + i // 2, 4) * 8 + ahead
                copy(src.at[slot(to)], dst.at[s], n, to, c).start()
            return 0

        lax.fori_loop(1 if steps == (0,) else 0, 8, body, 0, unroll=True)

    def exchange(src, dst, n, slot):
        for steps in ((2,), (1, 3), (0,)):
            exchange_part(src, dst, n, slot, steps)
        dst[s] = src[slot(s)]

    def whole(ref, count, n):
        part = ref.at[pl.ds(0, count)]
        return copy(part, part, n, s, c)

    def send_taps():
        for ahead in (2, 1, 3, 0):
            for y_step in range(4):
                if ahead or y_step:
                    chip = lax.rem(y_at + y_step, 4) * 4 + lax.rem(z_at + ahead, 4)
                    copy(send_h.at[chip], recv_h.at[half, f], 0, 2 * chip + half, c).start()
        recv_h[half, f] = send_h[f]

    def swap_taps():
        whole(recv_h.at[half], TAPS - 1, 0).wait_recv()
        return copy(recv_h.at[half], recv_h.at[half], 7, 2 * f + 1 - half, c)

    def send_inner():
        exchange(send_x, recv_x, 1, lambda to: to)

    def send_upstream():
        exchange_part(send_u, recv_u, 2, lambda to: to, (2,))
        swap = swap_taps()
        swap.start()
        exchange_part(send_u, recv_u, 2, lambda to: to, (1, 3))
        exchange_part(send_u, recv_u, 2, lambda to: to, (0,))
        recv_u[s] = send_u[s]
        return swap

    def take_taps(swap):
        swap.wait()
        toeplitz(recv_h, w)

    def take_inner():
        whole(recv_x, SEQ - 1, 1).wait_recv()
        spread_x(unpack(recv_x), xs)

    def take_upstream():
        whole(recv_u, SEQ - 1, 2).wait_recv()
        ut[...] = nt(eye(ROWS), unpack(recv_u).astype(BF16)).astype(BF16)

    def forward():
        convolve(xs, w, y)
        send_c[...] = pack(y[...])
        exchange(send_c, recv_c, 3, lambda to: to)

    def backward():
        spread_u(unpack(recv_u), us)
        convolve_back(us, w, y)
        send_b[...] = pack(y[...])

    def send_backward_far():
        exchange_part(send_b, recv_b, 4, lambda to: to, (2,))

    def send_backward_near():
        exchange_part(send_b, recv_b, 4, lambda to: to, (1, 3))
        exchange_part(send_b, recv_b, 4, lambda to: to, (0,))
        recv_b[s] = send_b[s]

    def correlation():
        correlate(ut, xs, send_g)

        def parts_out(i, _):
            to = lax.rem(c + i, CHAN)
            here = c * 2 + half

            @pl.when(i > 0)
            def _():
                copy(send_g.at[2 + 16 * half + to], recv_g.at[here], 5, s, to).start()

            other = 1 - half
            copy(send_g.at[2 + 16 * other + to], recv_g.at[here], 5, 2 * f + other, to).start()
            return 0

        lax.fori_loop(0, CHAN, parts_out, 0, unroll=True)
        recv_g[c * 2 + half] = send_g[2 + own_part]

    def totals():
        whole(recv_g, SEQ - 1, 5).wait_recv()
        send_t[0] = jnp.sum(recv_g[...], axis=0).astype(BF16)

        def total_out(i, _):
            to = lax.rem(c + i, CHAN)

            @pl.when(jnp.logical_not(jnp.logical_and(is_self, i == 0)))
            def _():
                copy(send_t.at[0], recv_t.at[f], 6, own_part, to).start()

            return 0

        lax.fori_loop(0, CHAN, total_out, 0, unroll=True)

        @pl.when(is_self)
        def _():
            recv_t[f] = send_t[0]

    send_taps()
    send_inner()
    swap = send_upstream()
    take_taps(swap)
    take_inner()
    forward()
    take_upstream()
    correlation()
    backward()
    send_backward_far()
    totals()
    send_backward_near()

    whole(recv_c, SEQ - 1, 3).wait_recv()
    tokens = nt(eye(LANES), recv_c[...].reshape(512, LANES)).astype(BF16)
    result = nn(tokens, route[...])
    for n in range(4):
        sums[pl.ds(LANES * (n ^ 1), LANES), :] = result[:, LANES * n : LANES * (n + 1)].astype(BF16)

    whole(recv_b, SEQ - 1, 4).wait_recv()
    tokens = nt(flip(LANES), recv_b[...].reshape(512, LANES)).astype(BF16)
    result = nn(tokens, route[...])
    for n in range(4):
        sums[pl.ds(512 + LANES * n, LANES), :] = result[:, LANES * n : LANES * (n + 1)].astype(BF16)

    @pl.when(is_self)
    def _():
        whole(recv_t, TAPS - 1, 6).wait()

    @pl.when(jnp.logical_not(is_self))
    def _():
        whole(recv_t, TAPS, 6).wait()

    grads[...] = recv_t[...]
    whole(recv_h.at[half], TAPS - 1, 0).wait_send()
    for n, ref in ((1, recv_x), (2, recv_u), (3, recv_c), (4, recv_b), (5, recv_g)):
        whole(ref, SEQ - 1, n).wait_send()


def finish(
    sums_far, grads_far, og_far, ig_far, va_far, ct_far,
    layer_out, outer_grad, inner_grad, value_grad, filter_grad,
    sums, grads, og, ig, va, ct, out_0, out_1, out_2, out_3, out_4, fetched, stored,
):
    sources = (grads_far, sums_far, og_far, ct_far, va_far, ig_far)
    fetches = [
        pltpu.make_async_copy(far, near, fetched.at[n])
        for n, (far, near) in enumerate(zip(sources, (grads, sums, og, ct, va, ig)))
    ]
    results = (layer_out, outer_grad, inner_grad, value_grad, filter_grad)
    stores = [
        pltpu.make_async_copy(near, far, stored.at[n])
        for n, (near, far) in enumerate(zip((out_0, out_1, out_2, out_3, out_4), results))
    ]
    for fetch in fetches:
        fetch.start()
    scale = float(512 * SEQ * LANES * CHAN // TAPS) ** -0.5
    fetches[0].wait()
    for n in range(4):
        out_4[:, LANES * n : LANES * (n + 1)] = nn(grads[:, n, :], flip(LANES)) * scale
    stores[4].start()
    fetches[1].wait()
    for n, (gate, out) in enumerate(((og, out_0), (ct, out_1), (va, out_2), (ig, out_3))):
        fetches[2 + n].wait()
        half = sums[512 * (n // 2) : 512 * (n // 2 + 1)]
        out[...] = (gate[...].astype(F32) * half.astype(F32)).astype(BF16)
        stores[n].start()
    for store in stores:
        store.wait()


def on_device(outer_gate, inner_gate, values, filters, cotangent):
    wide = jax.ShapeDtypeStruct((512, LANES), BF16)
    slots = pltpu.VMEM((SEQ, 16, LANES), BF16)
    near = pltpu.VMEM((512, LANES), BF16)
    vmem = pl.BlockSpec(memory_space=pltpu.VMEM)
    sums, grads = pl.pallas_call(
        kernel,
        out_shape=(
            jax.ShapeDtypeStruct((1024, LANES), BF16),
            jax.ShapeDtypeStruct((TAPS, 4, LANES), BF16),
        ),
        in_specs=[pl.BlockSpec(memory_space=pltpu.HBM)] * 5,
        out_specs=(vmem,) * 2,
        scratch_shapes=[
            pltpu.VMEM((TAPS, 4, LANES), BF16),
            slots, slots, slots, slots,
            pltpu.VMEM((2 + SEQ, 4, LANES), F32),
            pltpu.VMEM((1, 4, LANES), BF16),
            pltpu.VMEM((2, TAPS, 4, LANES), BF16),
            slots, slots, slots, slots,
            pltpu.VMEM((SEQ, 4, LANES), F32),
            pltpu.VMEM((TAPS, 4, LANES), BF16),
            near, near, near,
            pltpu.VMEM((TAPS, 512), BF16),
            near,
            pltpu.VMEM((129 * LANES, LANES), BF16),
            pltpu.VMEM((2 * ROWS, 1024), BF16),
            pltpu.VMEM((ROWS + 64, 1024), BF16),
            pltpu.VMEM((ROWS, ROWS), BF16),
            pltpu.VMEM((ROWS, ROWS), F32),
            pltpu.VMEM((512, 512), BF16),
            pltpu.SemaphoreType.DMA((8,)),
            pltpu.SemaphoreType.DMA((8,)),
            pltpu.SemaphoreType.DMA((5,)),
        ],
        compiler_params=pltpu.CompilerParams(
            collective_id=0, has_side_effects=True, vmem_limit_bytes=62 * 2**20
        ),
    )(outer_gate, inner_gate, values, filters.T, cotangent)
    *wides, filter_grad = pl.pallas_call(
        finish,
        out_shape=(wide, wide, wide, wide, jax.ShapeDtypeStruct((TAPS, 512), F32)),
        in_specs=[pl.BlockSpec(memory_space=pl.ANY)] * 6,
        out_specs=(pl.BlockSpec(memory_space=pl.ANY),) * 5,
        scratch_shapes=[
            pltpu.VMEM((1024, LANES), BF16),
            pltpu.VMEM((TAPS, 4, LANES), BF16),
            *[near] * 8,
            pltpu.VMEM((TAPS, 512), F32),
            pltpu.SemaphoreType.DMA((6,)),
            pltpu.SemaphoreType.DMA((5,)),
        ],
        compiler_params=pltpu.CompilerParams(vmem_limit_bytes=62 * 2**20),
    )(sums, grads, outer_gate, inner_gate, values, cotangent)
    return (*wides, filter_grad.T)


def solution(mesh):
    placed = (P("seq", "chan"),) * 3 + (P("seq", None), P("seq", "chan"))
    return jax.shard_map(
        on_device,
        mesh=mesh,
        in_specs=placed,
        out_specs=(P("seq", "chan"),) * 4 + (P("seq", None),),
        check_vma=False,
    )
```
